1024 devices in a mesh: dp: 64 (over y, z_lo, core), tensor: 16 (over z_hi, x).
Axes of the slice: x: 4, y: 4, z: 32 (z_hi: 4, z_lo: 8; z = z_hi * 8 + z_lo), core: 2. Of those that a mesh axis runs over, the one named last changes fastest.
Arguments:
- pre_act: bfloat16 [16384, 6912], P('dp', 'tensor'), may hold values from -6 to 6
- weight_out: bfloat16 [2560, 6912], P('dp', 'tensor'), may hold values from -0.21875 to 0.21875
- cotangent: bfloat16 [16384, 2560], P('dp'), may hold values from -16 to 16
Outputs:
- output: bfloat16 [16384, 2560], P('dp', 'tensor')
- grad_pre: bfloat16 [16384, 6912], P('dp', 'tensor')
- grad_weight: float32 [2560, 6912], P('dp', 'tensor')
The draws below stay inside these ranges and needn't reach their ends.
All inputs are finite; a program needn't handle non-finite values.
Results may differ from the reference program's by a relative error of at most 0.018.
Values may be sent and summed in bfloat16 or wider, within the bound.
No kernel may reach another device: no remote copies, remote signals or barrier semaphores. Data moves between devices by JAX's collectives and lax.ppermute only.
A program may use at most 32 MiB of HBM per device.

```python
import math
import jax
import jax.numpy as jnp
from jax import lax

D = 2560
FF = 6912
TOKENS = 16384
N_TENSOR = 16


def strengthened(entries, key, source, target, parts, factor):
    def block_of(axis_at):
        return (jnp.arange(entries.shape[axis_at]) // (entries.shape[axis_at] // parts)).reshape((-1,) + (1,) * (entries.ndim - 1 - axis_at))

    one_side = jax.random.permutation(key, parts)[block_of(target)]
    second = (block_of(target) + parts // 2) % parts
    return jnp.where((block_of(source) == one_side) | (block_of(source) == second), factor * entries, entries)


def block_levels(rng, shape, shards, smallest, top_value):
    def one(axis_at, parts):
        steps = jax.random.uniform(jax.random.fold_in(jax.random.fold_in(rng, 6), axis_at), (parts,), jnp.float32, smallest / len(shards), top_value / len(shards))
        return jnp.repeat(jnp.exp(steps), shape[axis_at] // parts).reshape((-1,) + (1,) * (len(shape) - axis_at - 1))

    level = one(*shards[0])
    for cut in shards[1:]:
        level = level * one(*cut)
    return level


def gaussian(key, extent, width, limit, cuts=(), dtype=jnp.bfloat16):
    array = width * jax.random.normal(key, extent, jnp.float32)
    if cuts:
        array = array * block_levels(key, extent, cuts, -0.22, 0.18)
    return jnp.clip(array, -limit, limit).astype(dtype)


def gaussian_with(own_key, dims, spread, reach, pieces, heavy, held_as=jnp.bfloat16):
    entries = spread * jax.random.normal(own_key, dims, jnp.float32)
    if pieces:
        entries = entries * block_levels(own_key, dims, pieces, -0.22, 0.18)
    return jnp.clip(strengthened(entries, jax.random.fold_in(own_key, 3), *heavy), -reach, reach).astype(held_as)


def setup_inputs(seed: int = 0) -> dict:
    seeds = jax.random.split(jax.random.key(seed), 4)
    return {
        "pre_act": gaussian(seeds[0], (TOKENS, FF), 1.0, 6.0, ((0, 64), (1, 16))),
        "weight_out": gaussian_with(seeds[1], (D, FF), FF ** -0.5, 0.21875, ((0, 64), (1, 16)), (1, 0, 64, 4.0)),
        "cotangent": gaussian_with(seeds[2], (TOKENS, D), 1.0, 16.0, ((0, 64),), (0, 1, 64, 4.0)),
    }


def gelu_value(values):
    inner = math.sqrt(2.0 / math.pi) * (values + 0.044715 * values * values * values)
    return 0.5 * values * (1.0 + jnp.tanh(inner))

def gelu_slope(values):
    coeff = math.sqrt(2.0 / math.pi)
    tangent = jnp.tanh(coeff * (values + 0.044715 * values * values * values))
    return 0.5 * (1.0 + tangent) + 0.5 * values * (1.0 - tangent * tangent) * coeff * (1.0 + 3.0 * 0.044715 * values * values)

def reference(pre_act, weight_out, cotangent):
    scaled = pre_act.astype(jnp.float32)
    hidden = gelu_value(scaled).astype(jnp.bfloat16)
    group = FF // N_TENSOR
    total = jnp.zeros((TOKENS, D), jnp.float32)
    for index in range(N_TENSOR):
        part_hidden = hidden[:, index * group:(index + 1) * group]
        part_weight = weight_out[:, index * group:(index + 1) * group]
        partial_value = lax.dot_general(part_hidden, part_weight, (((1,), (1,)), ((), ())), preferred_element_type=jnp.float32)
        partial_value = lax.optimization_barrier(partial_value.astype(jnp.bfloat16))
        total = total + partial_value.astype(jnp.float32)
    output = total.astype(jnp.bfloat16)
    grad_hidden = jnp.dot(cotangent, weight_out, preferred_element_type=jnp.float32)
    grad_pre = (grad_hidden * gelu_slope(scaled)).astype(jnp.bfloat16)
    grad_weight = lax.dot_general(cotangent, hidden, (((0,), (0,)), ((), ())), preferred_element_type=jnp.float32)
    grad_weight = grad_weight * (1.0 / math.sqrt(TOKENS))
    return (output, grad_pre, grad_weight)
```

```python
import math

import jax
import jax.numpy as jnp
import numpy as np
from jax import lax
from jax.sharding import Mesh, PartitionSpec as P

COEFF = math.sqrt(2.0 / math.pi)
AXES = ("y", "zl", "c", "zh", "x")
SIZES = (4, 8, 2, 4, 4)


def gelu_value(values):
    inner = COEFF * (values + 0.044715 * values * values * values)
    return 0.5 * values * (1.0 + jnp.tanh(inner))


def gelu_slope(values):
    tangent = jnp.tanh(COEFF * (values + 0.044715 * values * values * values))
    return 0.5 * (1.0 + tangent) + 0.5 * values * (1.0 - tangent * tangent) * COEFF * (
        1.0 + 3.0 * 0.044715 * values * values
    )


def swap(value, axis, distance):
    size = lax.axis_size(axis)
    return lax.ppermute(value, axis, [(i, i ^ distance) for i in range(size)])


def shift(value, axis, distance):
    size = lax.axis_size(axis)
    return lax.ppermute(value, axis, [(i, (i + distance) % size) for i in range(size)])


def dot(left, right, dims):
    return lax.dot_general(left, right, (dims, ((), ())), preferred_element_type=jnp.float32)


def selector(core, width, block):
    rows = lax.broadcasted_iota(jnp.int32, (2 * width, width), 0)
    cols = lax.broadcasted_iota(jnp.int32, (2 * width, width), 1)
    return (rows == cols // block * (2 * block) + core * block + cols % block).astype(jnp.bfloat16)


def local(pre_act, weight_out, cotangent):
    n_y, n_zl, n_x = lax.axis_size("y"), lax.axis_size("zl"), lax.axis_size("x")
    tokens, hid = pre_act.shape
    block = weight_out.shape[0]
    stripe = n_zl * block
    core, y, zl = lax.axis_index("c"), lax.axis_index("y"), lax.axis_index("zl")
    factor = 1.0 / math.sqrt(tokens * n_y * n_zl * 2)

    rows = weight_out[None]
    distance = n_zl // 2
    while distance:
        other = swap(rows, "zl", distance)
        low = (zl & distance) == 0
        first, second = jnp.where(low, rows, other), jnp.where(low, other, rows)
        rows = jnp.stack([first, second], axis=1).reshape(-1, block, hid)
        distance //= 2
    own = rows.reshape(n_x, stripe // n_x, hid)
    pieces = [own] + [shift(own, "y", -k) for k in range(1, n_y)]
    pieces = jnp.stack(pieces + pieces[:-1], axis=0)
    weight = lax.dynamic_slice_in_dim(pieces, (n_y - y) % n_y, n_y, axis=0)

    mine, theirs = [], []
    for index in range(n_y):
        part = cotangent[:, index * 2 * stripe : (index + 1) * 2 * stripe]
        mine.append(dot(part, selector(core, stripe, block), ((1,), (0,))).astype(jnp.bfloat16))
        theirs.append(dot(part, selector(1 - core, stripe, block), ((1,), (0,))).astype(jnp.bfloat16))
    mine, theirs = jnp.concatenate(mine, axis=1), jnp.concatenate(theirs, axis=1)
    pre_both = jnp.concatenate([pre_act, swap(pre_act, "c", 1)], axis=0)
    cot_both = jnp.concatenate([mine, swap(theirs, "c", 1)], axis=0)
    hidden = gelu_value(pre_both.astype(jnp.float32)).astype(jnp.bfloat16)

    term = dot(cot_both, hidden, ((0,), (0,))).astype(jnp.bfloat16)
    term = lax.all_to_all(term.reshape(n_y, stripe, hid), "y", 0, 0)
    term = jnp.sum(term.astype(jnp.float32), axis=0).astype(jnp.bfloat16)
    term = lax.all_to_all(term.reshape(n_zl, block, hid), "zl", 0, 0)
    grad_weight = jnp.sum(term.astype(jnp.float32), axis=0) * factor

    by_x = jnp.swapaxes(weight, 0, 1).reshape(n_y * stripe, hid)
    partial = dot(by_x, hidden, ((1,), (1,))).astype(jnp.bfloat16)
    partial = lax.all_to_all(partial.reshape(n_x, n_y * stripe // n_x, 2 * tokens), "x", 0, 0)
    partial = jnp.sum(partial.astype(jnp.float32), axis=0).astype(jnp.bfloat16)
    partial = lax.all_to_all(partial.reshape(n_y, stripe // n_x, 2 * tokens), "zh", 0, 0)
    summed = jnp.sum(partial.astype(jnp.float32), axis=0).astype(jnp.bfloat16)
    kept, given = summed[:, :tokens], swap(summed[:, tokens:], "c", 1)
    kept, given = kept.reshape(-1, 1, block, tokens), given.reshape(-1, 1, block, tokens)
    first, second = jnp.where(core == 0, kept, given), jnp.where(core == 0, given, kept)
    output = jnp.concatenate([first, second], axis=1).reshape(-1, tokens).T

    half = dot(cot_both, weight.reshape(-1, hid), ((1,), (0,)))
    grad_hidden = half[:tokens] + swap(half[tokens:], "c", 1)
    grad_pre = (grad_hidden * gelu_slope(pre_act.astype(jnp.float32))).astype(jnp.bfloat16)
    return (output, grad_pre, grad_weight)


def solution(mesh):
    fine = Mesh(np.asarray(mesh.devices).reshape(SIZES), AXES)
    dp, tensor = AXES[:3], AXES[3:]
    return jax.shard_map(
        local,
        mesh=fine,
        in_specs=(P(dp, tensor), P(dp, tensor), P(dp, None)),
        out_specs=(P(dp, tensor), P(dp, tensor), P(dp, tensor)),
        check_vma=False,
    )
```

```python
import functools
import math

import jax
import jax.numpy as jnp
import numpy as np
from jax import lax
from jax.experimental import pallas as pl
from jax.experimental.pallas import tpu as pltpu
from jax.sharding import Mesh, PartitionSpec as P

COEFF = math.sqrt(2.0 / math.pi)
AXES = ("y", "zl", "c", "zh", "x")
SIZES = (4, 8, 2, 4, 4)
F32, BF16 = jnp.float32, jnp.bfloat16
SMEM = pl.BlockSpec(memory_space=pltpu.SMEM)
VMEM = pl.BlockSpec(memory_space=pltpu.VMEM)
LATER = pl.BlockSpec(memory_space=pl.ANY)


def gelu_value(values):
    inner = COEFF * (values + 0.044715 * values * values * values)
    return 0.5 * values * (1.0 + jnp.tanh(inner))


def gelu_slope(values):
    tangent = jnp.tanh(COEFF * (values + 0.044715 * values * values * values))
    return 0.5 * (1.0 + tangent) + 0.5 * values * (1.0 - tangent * tangent) * COEFF * (
        1.0 + 3.0 * 0.044715 * values * values
    )


def swap(value, axis, distance):
    size = lax.axis_size(axis)
    return lax.ppermute(value, axis, [(i, i ^ distance) for i in range(size)])


def shift(value, axis, distance):
    size = lax.axis_size(axis)
    return lax.ppermute(value, axis, [(i, (i + distance) % size) for i in range(size)])


def dot(left, right, over_left, over_right):
    dims = (((over_left,), (over_right,)), ((), ()))
    return lax.dot_general(left, right, dims, preferred_element_type=F32)


def call(body, outs, specs, args, flops=0, scratch=()):
    moved = sum(a.size * a.dtype.itemsize for a in args) + sum(math.prod(s) * 2 for s, _ in outs)
    return pl.pallas_call(
        body,
        out_shape=[jax.ShapeDtypeStruct(s, d) for s, d in outs],
        in_specs=specs,
        out_specs=[VMEM] * len(outs),
        scratch_shapes=list(scratch),
        compiler_params=pltpu.CompilerParams(vmem_limit_bytes=14 << 20),
        cost_estimate=pl.CostEstimate(flops=flops, bytes_accessed=moved, transcendentals=0),
    )(*args)


def sort_channels(place, pick, cot, pre, send, mine):
    core, stripe = place[0], pick.shape[1]
    for index in range(cot.shape[1] // (2 * stripe)):
        part = cot[:, index * 2 * stripe : (index + 1) * 2 * stripe]
        rows = slice(index * stripe, (index + 1) * stripe)
        send[rows, :] = dot(pick[1 - core], part, 1, 1).astype(BF16)
        mine[rows, :] = dot(pick[core], part, 1, 1).astype(BF16)
    send[mine.shape[0] :, :] = pre[...]


def weight_term(pre, mine, got, after, hidden, term, *, stripe):
    tokens, channels = pre.shape[1], mine.shape[0]
    hidden[:, :tokens] = gelu_value(pre[...].astype(F32)).astype(BF16)
    hidden[:, tokens:] = gelu_value(got[channels:, :].astype(F32)).astype(BF16)
    for start in range(0, channels, stripe):
        rows = slice(start, start + stripe)
        total = dot(mine[rows, :], hidden[:, :tokens], 1, 1)
        total += dot(got[rows, :], hidden[:, tokens:], 1, 1)
        term[rows, :] = total.astype(BF16)


def sum_rounded(parts, after, then, last, out):
    total = parts[0].astype(F32)
    for index in range(1, parts.shape[0]):
        total += parts[index].astype(F32)
    out[...] = total.astype(out.dtype)


def sum_scaled(parts, after, out, *, factor):
    total = parts[0].astype(F32)
    for index in range(1, parts.shape[0]):
        total += parts[index].astype(F32)
    out[...] = total * factor


def order_rows(place, own, one, two, four, after, rows):
    zl = place[2]
    rows[zl] = own[...]
    rows[zl ^ 4] = one[...]
    for index, offset in enumerate((2, 6)):
        rows[zl ^ offset] = two[index]
    for index, offset in enumerate((1, 5, 3, 7)):
        rows[zl ^ offset] = four[index]


def output_terms(place, w0, w1, w2, w3, hidden, o0, o1, o2, o3, held):
    y, zh, x = place[1], place[3], place[4]
    group = held.shape[1]
    for k, piece in enumerate((w0, w1, w2, w3)):
        total = dot(piece[...], hidden[...], 1, 0).astype(BF16)
        for index in range(4):
            held[index] = total[index * group : (index + 1) * group]
        target = (y + k - zh + 4) % 4
        for r, out in enumerate((o0, o1, o2, o3)):
            out[target] = held[(x + r) % 4]


def sum_x(o0, g1, g2, g3, s0, s1, s3, left, right):
    def total(index):
        value = o0[index].astype(F32) + g1[index].astype(F32)
        return (value + (g2[index].astype(F32) + g3[index].astype(F32))).astype(BF16)

    half = left.shape[1]
    both = total(2)
    left[...] = both[:, :half]
    right[...] = both[:, half:]
    s0[...] = total(0)
    s1[...] = total(1)
    s3[...] = total(3)


def sum_step(s1, s3, left, right, t1, t3):
    half = left.shape[1]
    t1[:, :half] = (s1[:, :half].astype(F32) + left[...].astype(F32)).astype(BF16)
    t1[:, half:] = s1[:, half:]
    t3[:, :half] = s3[:, :half]
    t3[:, half:] = (s3[:, half:].astype(F32) + right[...].astype(F32)).astype(BF16)


def sum_last(s0, u, v, kept, given):
    half = kept.shape[1]
    total = (s0[...].astype(F32) + (u[...].astype(F32) + v[...].astype(F32))).astype(BF16)
    kept[...] = total[:, :half]
    given[...] = total[:, half:]


def hidden_terms(place, w0, w1, w2, w3, mine, got, own, other):
    y, stripe = place[1], w0.shape[0]
    own[...] = jnp.zeros_like(own)
    other[...] = jnp.zeros_like(other)
    for k, piece in enumerate((w0, w1, w2, w3)):
        rows = pl.ds(pl.multiple_of((y + k) % 4 * stripe, 16), stripe)
        own[...] += dot(piece[...], mine[rows, :], 0, 0)
        other[...] += dot(piece[...], got[rows, :], 0, 0)


def local(pick, pre_act, weight_out, cotangent):
    n_y, n_zl, n_x = SIZES[0], SIZES[1], SIZES[4]
    tokens, hid = pre_act.shape
    block = weight_out.shape[0]
    stripe = n_zl * block
    group = stripe // n_x
    channels = n_y * stripe
    core = lax.axis_index("c")
    place = jnp.stack([lax.axis_index(a) for a in ("c", "y", "zl", "zh", "x")]).astype(jnp.int32)
    factor = 1.0 / math.sqrt(tokens * n_y * n_zl * 2)
    work = 2 * tokens * channels * hid * 2
    pre = pre_act.T

    one = swap(weight_out, "zl", 4)
    send, mine = call(
        sort_channels,
        [((channels + hid, tokens), BF16), ((channels, tokens), BF16)],
        [SMEM, VMEM, VMEM, VMEM],
        (place, pick, cotangent, pre),
        flops=2 * 4 * tokens * stripe * stripe * 2 * 2,
    )
    got = swap(send, "c", 1)
    hidden, term = call(
        functools.partial(weight_term, stripe=stripe),
        [((hid, 2 * tokens), BF16), ((channels, hid), BF16)],
        [VMEM] * 3 + [LATER],
        (pre, mine, got, one),
        flops=work,
    )

    two = swap(jnp.stack([weight_out, one]), "zl", 2)
    four = swap(jnp.concatenate([weight_out[None], one[None], two]), "zl", 1)
    (rows,) = call(
        order_rows,
        [((n_zl, block, hid), BF16)],
        [SMEM] + [VMEM] * 4 + [LATER],
        (place, weight_out, one, two, four, term),
    )
    w0 = rows.reshape(stripe, hid)
    w1, w3, w2 = shift(w0, "y", -1), shift(w0, "y", 1), shift(w0, "y", 2)

    term = lax.all_to_all(term.reshape(n_y, stripe, hid), "y", 0, 0)
    (term,) = call(sum_rounded, [((stripe, hid), BF16)], [VMEM, LATER, LATER, LATER], (term, w1, w2, w3))
    term = lax.all_to_all(term.reshape(n_zl, block, hid), "zl", 0, 0)

    part = ((n_y, group, 2 * tokens), BF16)
    o0, o1, o2, o3 = call(
        output_terms,
        [part] * 4,
        [SMEM] + [VMEM] * 5,
        (place, w0, w1, w2, w3, hidden),
        flops=work,
        scratch=[pltpu.VMEM((n_x, group, 2 * tokens), BF16)],
    )
    g1, g3, g2 = shift(o1, "x", 1), shift(o3, "x", -1), shift(o2, "x", 2)
    whole, half = ((group, 2 * tokens), BF16), ((group, tokens), BF16)
    s0, s1, s3, left, right = call(
        sum_x, [whole] * 3 + [half] * 2, [VMEM] * 4, (o0, g1, g2, g3)
    )
    (grad_weight,) = call(
        functools.partial(sum_scaled, factor=factor), [((block, hid), F32)], [VMEM, LATER], (term, s0)
    )
    left, right = shift(left, "zh", 1), shift(right, "zh", -1)
    t1, t3 = call(sum_step, [whole] * 2, [VMEM] * 4, (s1, s3, left, right))
    u, v = shift(t1, "zh", 1), shift(t3, "zh", -1)
    kept, given = call(sum_last, [half] * 2, [VMEM] * 3, (s0, u, v))
    given = swap(given, "c", 1)
    kept, given = kept.reshape(-1, 1, block, tokens), given.reshape(-1, 1, block, tokens)
    first, second = jnp.where(core == 0, kept, given), jnp.where(core == 0, given, kept)
    output = jnp.concatenate([first, second], axis=1).reshape(-1, tokens).T

    own, other = call(
        hidden_terms,
        [((hid, tokens), F32)] * 2,
        [SMEM] + [VMEM] * 6,
        (place, w0, w1, w2, w3, mine, got),
        flops=work,
    )
    grad_hidden = own + swap(other, "c", 1)
    grad_pre = (grad_hidden * gelu_slope(pre.astype(F32))).astype(BF16).T
    return (output, grad_pre, grad_weight)


def solution(mesh):
    fine = Mesh(np.asarray(mesh.devices).reshape(SIZES), AXES)
    dp, tensor = AXES[:3], AXES[3:]
    mapped = jax.shard_map(
        local,
        mesh=fine,
        in_specs=(P(None, None, None), P(dp, tensor), P(dp, tensor), P(dp, None)),
        out_specs=(P(dp, tensor), P(dp, tensor), P(dp, tensor)),
        check_vma=False,
    )

    def run(pre_act, weight_out, cotangent):
        block = weight_out.shape[0] // (SIZES[0] * SIZES[1] * SIZES[2])
        stripe = SIZES[1] * block
        k = np.arange(stripe)
        table = np.zeros((2, stripe, 2 * stripe), np.float32)
        for core in range(2):
            table[core, k, k // block * (2 * block) + core * block + k % block] = 1.0
        return mapped(jnp.asarray(table, BF16), pre_act, weight_out, cotangent)

    return run
```

```python
import functools
import math

import jax
import jax.numpy as jnp
import numpy as np
from jax import lax
from jax.experimental import pallas as pl
from jax.experimental.pallas import tpu as pltpu
from jax.sharding import Mesh, PartitionSpec as P

COEFF = math.sqrt(2.0 / math.pi)
AXES = ("y", "zl", "c", "zh", "x")
SIZES = (4, 8, 2, 4, 4)
F32, BF16 = jnp.float32, jnp.bfloat16
SMEM = pl.BlockSpec(memory_space=pltpu.SMEM)
VMEM = pl.BlockSpec(memory_space=pltpu.VMEM)
LATER = pl.BlockSpec(memory_space=pl.ANY)


def gelu_value(values):
    inner = COEFF * (values + 0.044715 * values * values * values)
    return 0.5 * values * (1.0 + jnp.tanh(inner))


def gelu_slope(values):
    tangent = jnp.tanh(COEFF * (values + 0.044715 * values * values * values))
    return 0.5 * (1.0 + tangent) + 0.5 * values * (1.0 - tangent * tangent) * COEFF * (
        1.0 + 3.0 * 0.044715 * values * values
    )


def swap(value, axis, distance):
    size = lax.axis_size(axis)
    return lax.ppermute(value, axis, [(i, i ^ distance) for i in range(size)])


def shift(value, axis, distance):
    size = lax.axis_size(axis)
    return lax.ppermute(value, axis, [(i, (i + distance) % size) for i in range(size)])


def shift_both(value, distance):
    size = lax.axis_size("zh")
    pairs = [
        (core * size + i, core * size + (i + distance * (1 - 2 * core)) % size)
        for core in range(2)
        for i in range(size)
    ]
    return lax.ppermute(value, ("c", "zh"), pairs)


def dot(left, right, over_left, over_right):
    dims = (((over_left,), (over_right,)), ((), ()))
    return lax.dot_general(left, right, dims, preferred_element_type=F32)


def call(body, outs, specs, args, flops=0, scratch=()):
    moved = sum(a.size * a.dtype.itemsize for a in args) + sum(math.prod(s) * 2 for s, _ in outs)
    return pl.pallas_call(
        body,
        out_shape=[jax.ShapeDtypeStruct(s, d) for s, d in outs],
        in_specs=specs,
        out_specs=[VMEM] * len(outs),
        scratch_shapes=list(scratch),
        compiler_params=pltpu.CompilerParams(vmem_limit_bytes=14 << 20),
        cost_estimate=pl.CostEstimate(flops=flops, bytes_accessed=moved, transcendentals=0),
    )(*args)


def sort_channels(place, pick, cot, pre, after, send, mine):
    core, stripe = place[0], pick.shape[1]
    for index in range(cot.shape[1] // (2 * stripe)):
        part = cot[:, index * 2 * stripe : (index + 1) * 2 * stripe]
        rows = slice(index * stripe, (index + 1) * stripe)
        send[rows, :] = dot(pick[1 - core], part, 1, 1).astype(BF16)
        mine[rows, :] = dot(pick[core], part, 1, 1).astype(BF16)
    send[mine.shape[0] :, :] = pre[...]


def weight_term(pre, mine, got, hidden, term, *, stripe):
    tokens, channels = pre.shape[1], mine.shape[0]
    hidden[:, :tokens] = gelu_value(pre[...].astype(F32)).astype(BF16)
    hidden[:, tokens:] = gelu_value(got[channels:, :].astype(F32)).astype(BF16)
    for start in range(0, channels, stripe):
        rows = slice(start, start + stripe)
        total = dot(mine[rows, :], hidden[:, :tokens], 1, 1)
        total += dot(got[rows, :], hidden[:, tokens:], 1, 1)
        term[rows, :] = total.astype(BF16)


def split_y(place, parts, after, keep, send):
    bit = place[2] % 2

    def total(index):
        value = parts[0, index].astype(F32)
        for source in range(1, parts.shape[0]):
            value += parts[source, index].astype(F32)
        return value

    for index in range(keep.shape[0]):
        keep[index] = total(2 * index + bit)
        send[index] = total(2 * index + 1 - bit).astype(BF16)


def split_zl(place, kept, got, keep, send, *, width):
    bit = place[2] // width % 2
    for index in range(keep.shape[0]):
        near, far = 2 * index + bit, 2 * index + 1 - bit
        keep[index] = kept[near] + got[near].astype(F32)
        send[index] = (kept[far] + got[far].astype(F32)).astype(BF16)


def sum_scaled(kept, got, out, *, factor):
    out[...] = (kept[0] + got[0].astype(F32)) * factor


def order_rows(place, own, one, two, four, after, rows):
    zl = place[2]
    rows[zl] = own[...]
    rows[zl ^ 4] = one[...]
    for index, offset in enumerate((2, 6)):
        rows[zl ^ offset] = two[index]
    for index, offset in enumerate((1, 5, 3, 7)):
        rows[zl ^ offset] = four[index]


def output_terms(place, w0, w1, w2, w3, hidden, o0, o1, o2, o3, held):
    core, y, zh, x = place[0], place[1], place[3], place[4]
    group = held.shape[1]
    for k, piece in enumerate((w0, w1, w2, w3)):
        total = dot(piece[...], hidden[...], 1, 0).astype(BF16)
        for index in range(4):
            held[index] = total[index * group : (index + 1) * group]
        target = (y + k - zh + 4) * (1 + 2 * core) % 4
        for r, out in enumerate((o0, o1, o2, o3)):
            out[target] = held[(x + r) % 4]


def sum_x(o0, g1, g2, g3, after, s0, s1, s2, s3):
    for index, out in enumerate((s0, s1, s2, s3)):
        value = o0[index].astype(F32) + g1[index].astype(F32)
        out[...] = (value + (g2[index].astype(F32) + g3[index].astype(F32))).astype(BF16)


def sum_step(s1, got, after, t1):
    t1[...] = (s1[...].astype(F32) + got[...].astype(F32)).astype(BF16)


def sum_last(s0, u, v, after, kept, given):
    half = kept.shape[1]
    total = (s0[...].astype(F32) + (u[...].astype(F32) + v[...].astype(F32))).astype(BF16)
    kept[...] = total[:, :half]
    given[...] = total[:, half:]


def hidden_terms(place, w0, w1, w2, w3, mine, got, own, other):
    y, stripe = place[1], w0.shape[0]
    own[...] = jnp.zeros_like(own)
    other[...] = jnp.zeros_like(other)
    for k, piece in enumerate((w0, w1, w2, w3)):
        rows = pl.ds(pl.multiple_of((y + k) % 4 * stripe, 16), stripe)
        own[...] += dot(piece[...], mine[rows, :], 0, 0)
        other[...] += dot(piece[...], got[rows, :], 0, 0)


def local(pick, pre_act, weight_out, cotangent):
    n_y, n_zl, n_x = SIZES[0], SIZES[1], SIZES[4]
    tokens, hid = pre_act.shape
    block = weight_out.shape[0]
    stripe = n_zl * block
    group = stripe // n_x
    channels = n_y * stripe
    core = lax.axis_index("c")
    place = jnp.stack([lax.axis_index(a) for a in ("c", "y", "zl", "zh", "x")]).astype(jnp.int32)
    factor = 1.0 / math.sqrt(tokens * n_y * n_zl * 2)
    work = 2 * tokens * channels * hid * 2
    pre = pre_act.T

    one = swap(weight_out, "zl", 4)
    send, mine = call(
        sort_channels,
        [((channels + hid, tokens), BF16), ((channels, tokens), BF16)],
        [SMEM, VMEM, VMEM, VMEM, LATER],
        (place, pick, cotangent, pre, one),
        flops=2 * 4 * tokens * stripe * stripe * 2 * 2,
    )
    got = swap(send, "c", 1)
    hidden, term = call(
        functools.partial(weight_term, stripe=stripe),
        [((hid, 2 * tokens), BF16), ((channels, hid), BF16)],
        [VMEM] * 3,
        (pre, mine, got),
        flops=work,
    )

    two = swap(jnp.stack([weight_out, one]), "zl", 2)
    four = swap(jnp.concatenate([weight_out[None], one[None], two]), "zl", 1)
    (rows,) = call(
        order_rows,
        [((n_zl, block, hid), BF16)],
        [SMEM] + [VMEM] * 4 + [LATER],
        (place, weight_out, one, two, four, term),
    )
    w0 = rows.reshape(stripe, hid)
    w1, w3, w2 = shift(w0, "y", -1), shift(w0, "y", 1), shift(w0, "y", 2)

    term = lax.all_to_all(term.reshape(n_y, stripe, hid), "y", 0, 0)

    part = ((n_y, group, 2 * tokens), BF16)
    o0, o1, o2, o3 = call(
        output_terms,
        [part] * 4,
        [SMEM] + [VMEM] * 5,
        (place, w0, w1, w2, w3, hidden),
        flops=work,
        scratch=[pltpu.VMEM((n_x, group, 2 * tokens), BF16)],
    )
    g1, g3, g2 = shift(o1, "x", 1), shift(o3, "x", -1), shift(o2, "x", 2)
    own, other = call(
        hidden_terms,
        [((hid, tokens), F32)] * 2,
        [SMEM] + [VMEM] * 6,
        (place, w0, w1, w2, w3, mine, got),
        flops=work,
    )
    whole, half = ((group, 2 * tokens), BF16), ((group, tokens), BF16)
    quarter = n_zl // 2
    keep, send = call(
        split_y,
        [((quarter, block, hid), F32), ((quarter, block, hid), BF16)],
        [SMEM, VMEM, LATER],
        (place, term.reshape(n_y, n_zl, block, hid), own),
    )
    s0, s1, s2, s3 = call(sum_x, [whole] * 4, [VMEM] * 4 + [LATER], (o0, g1, g2, g3, keep))
    got2 = shift_both(s2, 1)
    keep, send = call(
        functools.partial(split_zl, width=2),
        [((quarter // 2, block, hid), F32), ((quarter // 2, block, hid), BF16)],
        [SMEM, VMEM, VMEM],
        (place, keep, swap(send, "zl", 1)),
    )
    (t1,) = call(sum_step, [whole], [VMEM] * 2 + [LATER], (s1, got2, keep))
    u, v = shift_both(t1, 1), shift_both(s3, -1)
    keep, send = call(
        functools.partial(split_zl, width=4),
        [((quarter // 4, block, hid), F32), ((quarter // 4, block, hid), BF16)],
        [SMEM, VMEM, VMEM],
        (place, keep, swap(send, "zl", 2)),
    )
    kept, given = call(sum_last, [half] * 2, [VMEM] * 3 + [LATER], (s0, u, v, keep))
    (grad_weight,) = call(
        functools.partial(sum_scaled, factor=factor),
        [((block, hid), F32)],
        [VMEM] * 2,
        (keep, swap(send, "zl", 4)),
    )
    given = swap(given, "c", 1)
    kept, given = kept.reshape(-1, 1, block, tokens), given.reshape(-1, 1, block, tokens)
    first, second = jnp.where(core == 0, kept, given), jnp.where(core == 0, given, kept)
    output = jnp.concatenate([first, second], axis=1).reshape(-1, tokens).T

    grad_hidden = own + swap(other, "c", 1)
    grad_pre = (grad_hidden * gelu_slope(pre.astype(F32))).astype(BF16).T
    return (output, grad_pre, grad_weight)


def solution(mesh):
    fine = Mesh(np.asarray(mesh.devices).reshape(SIZES), AXES)
    dp, tensor = AXES[:3], AXES[3:]
    mapped = jax.shard_map(
        local,
        mesh=fine,
        in_specs=(P(None, None, None), P(dp, tensor), P(dp, tensor), P(dp, None)),
        out_specs=(P(dp, tensor), P(dp, tensor), P(dp, tensor)),
        check_vma=False,
    )

    def run(pre_act, weight_out, cotangent):
        block = weight_out.shape[0] // (SIZES[0] * SIZES[1] * SIZES[2])
        stripe = SIZES[1] * block
        k = np.arange(stripe)
        table = np.zeros((2, stripe, 2 * stripe), np.float32)
        for core in range(2):
            table[core, k, k // block * (2 * block) + core * block + k % block] = 1.0
        return mapped(jnp.asarray(table, BF16), pre_act, weight_out, cotangent)

    return run
```

```python
import functools
import math

import jax
import jax.numpy as jnp
import numpy as np
from jax import lax
from jax.experimental import pallas as pl
from jax.experimental.pallas import tpu as pltpu
from jax.sharding import Mesh, PartitionSpec as P

COEFF = math.sqrt(2.0 / math.pi)
AXES = ("y", "zl", "c", "zh", "x")
SIZES = (4, 8, 2, 4, 4)
F32, BF16 = jnp.float32, jnp.bfloat16
SMEM = pl.BlockSpec(memory_space=pltpu.SMEM)
VMEM = pl.BlockSpec(memory_space=pltpu.VMEM)
LATER = pl.BlockSpec(memory_space=pl.ANY)
HBM = pl.BlockSpec(memory_space=pltpu.HBM)


def gelu_value(values):
    inner = COEFF * (values + 0.044715 * values * values * values)
    return 0.5 * values * (1.0 + jnp.tanh(inner))


def gelu_slope(values):
    tangent = jnp.tanh(COEFF * (values + 0.044715 * values * values * values))
    return 0.5 * (1.0 + tangent) + 0.5 * values * (1.0 - tangent * tangent) * COEFF * (
        1.0 + 3.0 * 0.044715 * values * values
    )


def swap(value, axis, distance):
    size = lax.axis_size(axis)
    return lax.ppermute(value, axis, [(i, i ^ distance) for i in range(size)])


def shift(value, axis, distance):
    size = lax.axis_size(axis)
    return lax.ppermute(value, axis, [(i, (i + distance) % size) for i in range(size)])


def shift_both(value, distance):
    size = lax.axis_size("zh")
    pairs = [
        (core * size + i, core * size + (i + distance * (1 - 2 * core)) % size)
        for core in range(2)
        for i in range(size)
    ]
    return lax.ppermute(value, ("c", "zh"), pairs)


def dot(left, right, over_left, over_right):
    dims = (((over_left,), (over_right,)), ((), ()))
    return lax.dot_general(left, right, dims, preferred_element_type=F32)


def call(body, outs, specs, args, flops=0, scratch=(), out_specs=None, limit=14):
    moved = sum(a.size * a.dtype.itemsize for a in args) + sum(a.size for a in args)
    return pl.pallas_call(
        body,
        out_shape=[s if isinstance(s, pl.MemoryRef) else jax.ShapeDtypeStruct(*s) for s in outs],
        in_specs=specs,
        out_specs=out_specs or [VMEM] * len(outs),
        scratch_shapes=list(scratch),
        compiler_params=pltpu.CompilerParams(vmem_limit_bytes=limit << 20),
        cost_estimate=pl.CostEstimate(flops=flops, bytes_accessed=moved, transcendentals=0),
    )(*args)


def sort_channels(place, base, cot, pre, send, mine, *, block):
    core, stripe = place[0], base.shape[0]
    lanes = lax.broadcasted_iota(jnp.int32, (stripe, 2 * stripe), 1)
    own = jnp.where(lanes == base[...] + core * block, 1.0, 0.0).astype(BF16)
    other = jnp.where(lanes == base[...] + (1 - core) * block, 1.0, 0.0).astype(BF16)
    for index in range(cot.shape[1] // (2 * stripe)):
        part = cot[:, index * 2 * stripe : (index + 1) * 2 * stripe]
        rows = slice(index * stripe, (index + 1) * stripe)
        send[rows, :] = dot(other, part, 1, 1).astype(BF16)
        mine[rows, :] = dot(own, part, 1, 1).astype(BF16)
    send[mine.shape[0] :, :] = pre[...]


def weight_term(pre, mine, got, after, hidden, term, both, held, sems, *, stripe):
    tokens, channels = pre.shape[1], mine.shape[0]
    copies = [
        pltpu.make_async_copy(mine, both.at[0], sems.at[0]),
        pltpu.make_async_copy(got.at[pl.ds(0, channels)], both.at[1], sems.at[1]),
    ]
    for copy in copies:
        copy.start()
    hidden[:, :tokens] = gelu_value(pre[...].astype(F32)).astype(BF16)
    hidden[:, tokens:] = gelu_value(got[channels:, :].astype(F32)).astype(BF16)
    for index in range(channels // stripe):
        rows = slice(index * stripe, (index + 1) * stripe)
        total = dot(mine[rows, :], hidden[:, :tokens], 1, 1)
        total += dot(got[rows, :], hidden[:, tokens:], 1, 1)
        held[index] = total.astype(BF16)
        copies.append(pltpu.make_async_copy(held.at[index], term.at[index], sems.at[2 + index]))
        copies[-1].start()
    for copy in copies:
        copy.wait()


def split_y(place, parts, after, keep, send):
    bit = place[2] % 2

    def total(index):
        value = parts[0, index].astype(F32)
        for source in range(1, parts.shape[0]):
            value += parts[source, index].astype(F32)
        return value

    for index in range(keep.shape[0]):
        keep[index] = total(2 * index + bit)
        send[index] = total(2 * index + 1 - bit).astype(BF16)


def split_zl(place, kept, got, keep, send, *, width):
    bit = place[2] // width % 2
    for index in range(keep.shape[0]):
        near, far = 2 * index + bit, 2 * index + 1 - bit
        keep[index] = kept[near] + got[near].astype(F32)
        send[index] = (kept[far] + got[far].astype(F32)).astype(BF16)


def sum_scaled(kept, got, out, *, factor):
    out[...] = (kept[0] + got[0].astype(F32)) * factor


def order_rows(place, own, one, two, four, after, rows):
    zl = place[2]
    rows[zl] = own[...]
    rows[zl ^ 4] = one[...]
    for index, offset in enumerate((2, 6)):
        rows[zl ^ offset] = two[index]
    for index, offset in enumerate((1, 5, 3, 7)):
        rows[zl ^ offset] = four[index]


def output_terms(place, w0, w1, w2, w3, hidden, out, weight, held, sems):
    core, y, zh = place[0], place[1], place[3]
    group = out.shape[2]
    pieces = (w0, w1, w2, w3)
    copies = [pltpu.make_async_copy(p, weight.at[k], sems.at[k]) for k, p in enumerate(pieces)]
    for copy in copies:
        copy.start()
    for k, piece in enumerate(pieces):
        total = dot(piece[...], hidden[...], 1, 0).astype(BF16)
        target = (y + k - zh + 4) * (1 + 2 * core) % 4
        for x in range(out.shape[0]):
            held[k, x] = total[x * group : (x + 1) * group]
        copies.append(pltpu.make_async_copy(held.at[k], out.at[:, target], sems.at[4 + k]))
        copies[-1].start()
    for copy in copies:
        copy.wait()


def sum_x(parts, after, s0, s1, s2, s3):
    for index, out in enumerate((s0, s1, s2, s3)):
        value = parts[0, index].astype(F32) + parts[1, index].astype(F32)
        value += parts[2, index].astype(F32) + parts[3, index].astype(F32)
        out[...] = value.astype(BF16)


def sum_step(s1, got, after, t1):
    t1[...] = (s1[...].astype(F32) + got[...].astype(F32)).astype(BF16)


def sum_last(s0, u, v, kept, given):
    half = kept.shape[1]
    total = (s0[...].astype(F32) + (u[...].astype(F32) + v[...].astype(F32))).astype(BF16)
    kept[...] = total[:, :half]
    given[...] = total[:, half:]


def gate(value, after, out):
    pass


def hold(value, after):
    return pl.pallas_call(
        gate,
        out_shape=pltpu.HBM(value.shape, value.dtype),
        in_specs=[HBM, LATER],
        out_specs=HBM,
        input_output_aliases={0: 0},
        compiler_params=pltpu.CompilerParams(vmem_limit_bytes=14 << 20),
    )(value, after)


def interleave(place, kept, given, out):
    core = place[0]
    for index in range(kept.shape[0]):
        out[index, core] = kept[index]
        out[index, 1 - core] = given[index]


def hidden_terms(place, weight, both, own, other):
    y, count, stripe = place[1], weight.shape[0], weight.shape[1]
    own[...] = jnp.zeros_like(own)
    other[...] = jnp.zeros_like(other)
    for k in range(count):
        rows = pl.ds(pl.multiple_of((y + k) % count * stripe, 16), stripe)
        own[...] += dot(weight[k], both[0, rows, :], 0, 0)
        other[...] += dot(weight[k], both[1, rows, :], 0, 0)


def local(base, pre_act, weight_out, cotangent):
    n_y, n_zl, n_x = SIZES[0], SIZES[1], SIZES[4]
    tokens, hid = pre_act.shape
    block = weight_out.shape[0]
    stripe = n_zl * block
    group = stripe // n_x
    channels = n_y * stripe
    place = jnp.stack([lax.axis_index(a) for a in ("c", "y", "zl", "zh", "x")]).astype(jnp.int32)
    factor = 1.0 / math.sqrt(tokens * n_y * n_zl * 2)
    work = 2 * tokens * channels * hid * 2
    pre = pre_act.T

    one = swap(weight_out, "zl", 4)
    first = jnp.stack([weight_out, one])
    send, mine = call(
        functools.partial(sort_channels, block=block),
        [((channels + hid, tokens), BF16), ((channels, tokens), BF16)],
        [SMEM, VMEM, VMEM, VMEM],
        (place, base, cotangent, pre),
        flops=2 * 4 * tokens * stripe * stripe * 2 * 2,
        limit=56,
    )
    two = swap(first, "zl", 2)
    second = jnp.concatenate([first, two])
    got = swap(hold(send, two), "c", 1)
    hidden, term, both = call(
        functools.partial(weight_term, stripe=stripe),
        [((hid, 2 * tokens), BF16), pltpu.HBM((n_y, stripe, hid), BF16), pltpu.HBM((2, channels, tokens), BF16)],
        [VMEM] * 3 + [LATER],
        (pre, mine, got, second),
        flops=work,
        scratch=[pltpu.VMEM((n_y, stripe, hid), BF16), pltpu.SemaphoreType.DMA((2 + n_y,))],
        out_specs=[VMEM, HBM, HBM],
    )

    four = swap(second, "zl", 1)
    (rows,) = call(
        order_rows,
        [((n_zl, block, hid), BF16)],
        [SMEM] + [VMEM] * 4 + [LATER],
        (place, weight_out, one, two, four, hidden),
    )
    w0 = rows.reshape(stripe, hid)
    w1, w3, w2 = shift(w0, "y", -1), shift(w0, "y", 1), shift(w0, "y", 2)

    term = lax.all_to_all(hold(term, rows), "y", 0, 0)

    parts, weight = call(
        output_terms,
        [pltpu.HBM((n_x, n_y, group, 2 * tokens), BF16), pltpu.HBM((n_y, stripe, hid), BF16)],
        [SMEM] + [VMEM] * 5,
        (place, w0, w1, w2, w3, hidden),
        flops=work,
        scratch=[pltpu.VMEM((n_y, n_x, group, 2 * tokens), BF16), pltpu.SemaphoreType.DMA((2 * n_y,))],
        out_specs=[HBM, HBM],
    )
    parts = lax.all_to_all(parts, "x", 0, 0)

    own, other = call(
        hidden_terms,
        [((hid, tokens), F32)] * 2,
        [SMEM, VMEM, VMEM],
        (place, weight, both),
        flops=work,
    )
    whole, half = ((group, 2 * tokens), BF16), ((group, tokens), BF16)
    quarter = n_zl // 2
    keep, send = call(
        split_y,
        [((quarter, block, hid), F32), ((quarter, block, hid), BF16)],
        [SMEM, VMEM, LATER],
        (place, term.reshape(n_y, n_zl, block, hid), own),
    )
    keep, send = call(
        functools.partial(split_zl, width=2),
        [((quarter // 2, block, hid), F32), ((quarter // 2, block, hid), BF16)],
        [SMEM, VMEM, VMEM],
        (place, keep, swap(send, "zl", 1)),
    )
    s0, s1, s2, s3 = call(sum_x, [whole] * 4, [VMEM, LATER], (parts, keep))
    got2 = shift_both(s2, 1)
    keep, send = call(
        functools.partial(split_zl, width=4),
        [((quarter // 4, block, hid), F32), ((quarter // 4, block, hid), BF16)],
        [SMEM, VMEM, VMEM],
        (place, keep, swap(send, "zl", 2)),
    )
    (t1,) = call(sum_step, [whole], [VMEM] * 2 + [LATER], (s1, got2, keep))
    u, v = shift_both(t1, 1), shift_both(s3, -1)
    kept, given = call(sum_last, [half] * 2, [VMEM] * 3, (s0, u, v))
    (grad_weight,) = call(
        functools.partial(sum_scaled, factor=factor),
        [((block, hid), F32)],
        [VMEM] * 2,
        (keep, swap(send, "zl", 4)),
    )
    given = swap(given, "c", 1)
    (output,) = call(
        interleave,
        [((group // block, 2, block, tokens), BF16)],
        [SMEM, VMEM, VMEM],
        (place, kept.reshape(-1, block, tokens), given.reshape(-1, block, tokens)),
    )
    output = output.reshape(-1, tokens).T
    grad_hidden = own + swap(other, "c", 1)
    grad_pre = (grad_hidden * gelu_slope(pre.astype(F32))).astype(BF16).T
    return (output, grad_pre, grad_weight)


def solution(mesh):
    fine = Mesh(np.asarray(mesh.devices).reshape(SIZES), AXES)
    dp, tensor = AXES[:3], AXES[3:]
    mapped = jax.shard_map(
        local,
        mesh=fine,
        in_specs=(P(None, None), P(dp, tensor), P(dp, tensor), P(dp, None)),
        out_specs=(P(dp, tensor), P(dp, tensor), P(dp, tensor)),
        check_vma=False,
    )

    def run(pre_act, weight_out, cotangent):
        block = weight_out.shape[0] // (SIZES[0] * SIZES[1] * SIZES[2])
        k = np.arange(SIZES[1] * block)
        base = (k // block * (2 * block) + k % block).astype(np.int32)[:, None]
        return mapped(jnp.asarray(base), pre_act, weight_out, cotangent)

    return run
```

```python
import functools
import math

import jax
import jax.numpy as jnp
import numpy as np
from jax import lax
from jax.experimental import pallas as pl
from jax.experimental.pallas import tpu as pltpu
from jax.sharding import Mesh, PartitionSpec as P

COEFF = math.sqrt(2.0 / math.pi)
AXES = ("y", "zl", "c", "zh", "x")
SIZES = (4, 8, 2, 4, 4)
F32, BF16 = jnp.float32, jnp.bfloat16
SMEM = pl.BlockSpec(memory_space=pltpu.SMEM)
VMEM = pl.BlockSpec(memory_space=pltpu.VMEM)
LATER = pl.BlockSpec(memory_space=pl.ANY)
HBM = pl.BlockSpec(memory_space=pltpu.HBM)


def gelu_value(values):
    inner = COEFF * (values + 0.044715 * values * values * values)
    return 0.5 * values * (1.0 + jnp.tanh(inner))


def gelu_slope(values):
    tangent = jnp.tanh(COEFF * (values + 0.044715 * values * values * values))
    return 0.5 * (1.0 + tangent) + 0.5 * values * (1.0 - tangent * tangent) * COEFF * (
        1.0 + 3.0 * 0.044715 * values * values
    )


def swap(value, axis, distance):
    size = lax.axis_size(axis)
    return lax.ppermute(value, axis, [(i, i ^ distance) for i in range(size)])


def shift(value, axis, distance):
    size = lax.axis_size(axis)
    return lax.ppermute(value, axis, [(i, (i + distance) % size) for i in range(size)])


def shift_both(value, distance):
    size = lax.axis_size("zh")
    pairs = [
        (core * size + i, core * size + (i + distance * (1 - 2 * core)) % size)
        for core in range(2)
        for i in range(size)
    ]
    return lax.ppermute(value, ("c", "zh"), pairs)


def dot(left, right, over_left, over_right):
    dims = (((over_left,), (over_right,)), ((), ()))
    return lax.dot_general(left, right, dims, preferred_element_type=F32)


def call(body, outs, specs, args, flops=0, scratch=(), out_specs=None, limit=14):
    moved = sum(a.size * a.dtype.itemsize for a in args) + sum(a.size for a in args)
    return pl.pallas_call(
        body,
        out_shape=[s if isinstance(s, pl.MemoryRef) else jax.ShapeDtypeStruct(*s) for s in outs],
        in_specs=specs,
        out_specs=out_specs or [VMEM] * len(outs),
        scratch_shapes=list(scratch),
        compiler_params=pltpu.CompilerParams(vmem_limit_bytes=limit << 20),
        cost_estimate=pl.CostEstimate(flops=flops, bytes_accessed=moved, transcendentals=0),
    )(*args)


def sort_channels(place, base, cot, pre, send, mine, *, block):
    core, stripe = place[0], base.shape[0]
    lanes = lax.broadcasted_iota(jnp.int32, (stripe, 2 * stripe), 1)
    own = jnp.where(lanes == base[...] + core * block, 1.0, 0.0).astype(BF16)
    other = jnp.where(lanes == base[...] + (1 - core) * block, 1.0, 0.0).astype(BF16)
    for index in range(cot.shape[1] // (2 * stripe)):
        part = cot[:, index * 2 * stripe : (index + 1) * 2 * stripe]
        rows = slice(index * stripe, (index + 1) * stripe)
        send[rows, :] = dot(other, part, 1, 1).astype(BF16)
        mine[rows, :] = dot(own, part, 1, 1).astype(BF16)
    send[mine.shape[0] :, :] = pre[...]


def weight_term(place, pre, mine, got, after, hidden, t0, t1, t2, t3, both, held, sems, *, stripe):
    y, tokens, channels = place[1], pre.shape[1], mine.shape[0]
    copies = [
        pltpu.make_async_copy(mine, both.at[0], sems.at[0]),
        pltpu.make_async_copy(got.at[pl.ds(0, channels)], both.at[1], sems.at[1]),
    ]
    for copy in copies:
        copy.start()
    hidden[:, :tokens] = gelu_value(pre[...].astype(F32)).astype(BF16)
    hidden[:, tokens:] = gelu_value(got[channels:, :].astype(F32)).astype(BF16)
    for index, term in enumerate((t0, t1, t2, t3)):
        rows = pl.ds(pl.multiple_of((y + index) % 4 * stripe, 16), stripe)
        total = dot(mine[rows, :], hidden[:, :tokens], 1, 1)
        total += dot(got[rows, :], hidden[:, tokens:], 1, 1)
        held[index] = total.astype(BF16)
        copies.append(pltpu.make_async_copy(held.at[index], term, sems.at[2 + index]))
        copies[-1].start()
    for copy in copies:
        copy.wait()


def split_y(place, p0, p1, p2, p3, after, keep, send):
    bit = place[2] % 2

    def total(index):
        value = p0[index].astype(F32) + p1[index].astype(F32)
        return value + (p2[index].astype(F32) + p3[index].astype(F32))

    for index in range(keep.shape[0]):
        keep[index] = total(2 * index + bit)
        send[index] = total(2 * index + 1 - bit).astype(BF16)


def split_zl(place, kept, got, keep, send, *, width):
    bit = place[2] // width % 2
    for index in range(keep.shape[0]):
        near, far = 2 * index + bit, 2 * index + 1 - bit
        keep[index] = kept[near] + got[near].astype(F32)
        send[index] = (kept[far] + got[far].astype(F32)).astype(BF16)


def sum_scaled(kept, got, out, *, factor):
    out[...] = (kept[0] + got[0].astype(F32)) * factor


def order_rows(place, own, one, two, four, after, rows):
    zl = place[2]
    rows[zl] = own[...]
    rows[zl ^ 4] = one[...]
    for index, offset in enumerate((2, 6)):
        rows[zl ^ offset] = two[index]
    for index, offset in enumerate((1, 5, 3, 7)):
        rows[zl ^ offset] = four[index]


def output_terms(place, w0, w1, w2, w3, hidden, out, weight, held, sems):
    core, y, zh = place[0], place[1], place[3]
    group = out.shape[2]
    pieces = (w0, w1, w2, w3)
    copies = [pltpu.make_async_copy(p, weight.at[k], sems.at[k]) for k, p in enumerate(pieces)]
    for copy in copies:
        copy.start()
    for k, piece in enumerate(pieces):
        total = dot(piece[...], hidden[...], 1, 0).astype(BF16)
        target = (y + k - zh + 4) * (1 + 2 * core) % 4
        for x in range(out.shape[0]):
            held[k, x] = total[x * group : (x + 1) * group]
        copies.append(pltpu.make_async_copy(held.at[k], out.at[:, target], sems.at[4 + k]))
        copies[-1].start()
    for copy in copies:
        copy.wait()


def sum_x(parts, after, s0, s1, s2, s3):
    for index, out in enumerate((s0, s1, s2, s3)):
        value = parts[0, index].astype(F32) + parts[1, index].astype(F32)
        value += parts[2, index].astype(F32) + parts[3, index].astype(F32)
        out[...] = value.astype(BF16)


def sum_step(s1, got, t1):
    t1[...] = (s1[...].astype(F32) + got[...].astype(F32)).astype(BF16)


def sum_last(s0, u, v, after, then, kept, given):
    half = kept.shape[1]
    total = (s0[...].astype(F32) + (u[...].astype(F32) + v[...].astype(F32))).astype(BF16)
    kept[...] = total[:, :half]
    given[...] = total[:, half:]


def gate(value, after, out):
    pass


def hold(value, after, place=LATER):
    return pl.pallas_call(
        gate,
        out_shape=pltpu.HBM(value.shape, value.dtype),
        in_specs=[HBM, place],
        out_specs=HBM,
        input_output_aliases={0: 0},
        compiler_params=pltpu.CompilerParams(vmem_limit_bytes=14 << 20),
    )(value, after)


def interleave(place, kept, given, out):
    core = place[0]
    for index in range(kept.shape[0]):
        out[index, core] = kept[index]
        out[index, 1 - core] = given[index]


def hidden_terms(place, weight, both, own, other):
    y, count, stripe = place[1], weight.shape[0], weight.shape[1]
    own[...] = jnp.zeros_like(own)
    other[...] = jnp.zeros_like(other)
    for k in range(count):
        rows = pl.ds(pl.multiple_of((y + k) % count * stripe, 16), stripe)
        own[...] += dot(weight[k], both[0, rows, :], 0, 0)
        other[...] += dot(weight[k], both[1, rows, :], 0, 0)


def local(base, pre_act, weight_out, cotangent):
    n_y, n_zl, n_x = SIZES[0], SIZES[1], SIZES[4]
    tokens, hid = pre_act.shape
    block = weight_out.shape[0]
    stripe = n_zl * block
    group = stripe // n_x
    channels = n_y * stripe
    place = jnp.stack([lax.axis_index(a) for a in ("c", "y", "zl", "zh", "x")]).astype(jnp.int32)
    factor = 1.0 / math.sqrt(tokens * n_y * n_zl * 2)
    work = 2 * tokens * channels * hid * 2
    pre = pre_act.T

    one = swap(weight_out, "zl", 4)
    first = jnp.stack([weight_out, one])
    send, mine = call(
        functools.partial(sort_channels, block=block),
        [((channels + hid, tokens), BF16), ((channels, tokens), BF16)],
        [SMEM, VMEM, VMEM, VMEM],
        (place, base, cotangent, pre),
        flops=2 * 4 * tokens * stripe * stripe * 2 * 2,
        limit=56,
    )
    two = swap(first, "zl", 2)
    second = jnp.concatenate([first, two])
    got = swap(hold(send, two), "c", 1)
    hidden, t0, t1, t2, t3, both = call(
        functools.partial(weight_term, stripe=stripe),
        [((hid, 2 * tokens), BF16)]
        + [pltpu.HBM((stripe, hid), BF16)] * n_y
        + [pltpu.HBM((2, channels, tokens), BF16)],
        [SMEM] + [VMEM] * 3 + [LATER],
        (place, pre, mine, got, second),
        flops=work,
        scratch=[pltpu.VMEM((n_y, stripe, hid), BF16), pltpu.SemaphoreType.DMA((2 + n_y,))],
        out_specs=[VMEM] + [HBM] * (n_y + 1),
    )

    four = swap(second, "zl", 1)
    (rows,) = call(
        order_rows,
        [((n_zl, block, hid), BF16)],
        [SMEM] + [VMEM] * 4 + [LATER],
        (place, weight_out, one, two, four, hidden),
    )
    w0 = rows.reshape(stripe, hid)
    w1, w3, w2 = shift(w0, "y", -1), shift(w0, "y", 1), shift(w0, "y", 2)

    parts, weight = call(
        output_terms,
        [pltpu.HBM((n_x, n_y, group, 2 * tokens), BF16), pltpu.HBM((n_y, stripe, hid), BF16)],
        [SMEM] + [VMEM] * 5,
        (place, w0, w1, w2, w3, hidden),
        flops=work,
        scratch=[pltpu.VMEM((n_y, n_x, group, 2 * tokens), BF16), pltpu.SemaphoreType.DMA((2 * n_y,))],
        out_specs=[HBM, HBM],
    )
    t1, t2, t3 = (shift(hold(t, parts, HBM), "y", k) for k, t in ((1, t1), (2, t2), (3, t3)))
    parts = lax.all_to_all(parts, "x", 0, 0)

    whole, half = ((group, 2 * tokens), BF16), ((group, tokens), BF16)
    quarter = n_zl // 2
    terms = [t.reshape(n_zl, block, hid) for t in (t0, t1, t2, t3)]
    s0, s1, s2, s3 = call(sum_x, [whole] * 4, [VMEM, LATER], (parts, terms[3]))
    got2 = shift_both(s2, 1)
    (s1,) = call(sum_step, [whole], [VMEM] * 2, (s1, got2))
    u, v = shift_both(s1, 1), shift_both(s3, -1)
    keep, send = call(
        split_y,
        [((quarter, block, hid), F32), ((quarter, block, hid), BF16)],
        [SMEM] + [VMEM] * 4 + [LATER],
        (place, *terms, s1),
    )
    own, other = call(
        hidden_terms,
        [((hid, tokens), F32)] * 2,
        [SMEM, VMEM, VMEM],
        (place, weight, both),
        flops=work,
    )
    keep, send = call(
        functools.partial(split_zl, width=2),
        [((quarter // 2, block, hid), F32), ((quarter // 2, block, hid), BF16)],
        [SMEM, VMEM, VMEM],
        (place, keep, swap(send, "zl", 1)),
    )
    kept, given = call(sum_last, [half] * 2, [VMEM] * 3 + [LATER] * 2, (s0, u, v, keep, own))
    keep, send = call(
        functools.partial(split_zl, width=4),
        [((quarter // 4, block, hid), F32), ((quarter // 4, block, hid), BF16)],
        [SMEM, VMEM, VMEM],
        (place, keep, swap(send, "zl", 2)),
    )
    (grad_weight,) = call(
        functools.partial(sum_scaled, factor=factor),
        [((block, hid), F32)],
        [VMEM] * 2,
        (keep, swap(send, "zl", 4)),
    )
    given = swap(given, "c", 1)
    (output,) = call(
        interleave,
        [((group // block, 2, block, tokens), BF16)],
        [SMEM, VMEM, VMEM],
        (place, kept.reshape(-1, block, tokens), given.reshape(-1, block, tokens)),
    )
    output = output.reshape(-1, tokens).T
    grad_hidden = own + swap(other, "c", 1)
    grad_pre = (grad_hidden * gelu_slope(pre.astype(F32))).astype(BF16).T
    return (output, grad_pre, grad_weight)


def solution(mesh):
    fine = Mesh(np.asarray(mesh.devices).reshape(SIZES), AXES)
    dp, tensor = AXES[:3], AXES[3:]
    mapped = jax.shard_map(
        local,
        mesh=fine,
        in_specs=(P(None, None), P(dp, tensor), P(dp, tensor), P(dp, None)),
        out_specs=(P(dp, tensor), P(dp, tensor), P(dp, tensor)),
        check_vma=False,
    )

    def run(pre_act, weight_out, cotangent):
        block = weight_out.shape[0] // (SIZES[0] * SIZES[1] * SIZES[2])
        k = np.arange(SIZES[1] * block)
        base = (k // block * (2 * block) + k % block).astype(np.int32)[:, None]
        return mapped(jnp.asarray(base), pre_act, weight_out, cotangent)

    return run
```

```python
import functools
import math

import jax
import jax.numpy as jnp
import numpy as np
from jax import lax
from jax.experimental import pallas as pl
from jax.experimental.pallas import tpu as pltpu
from jax.sharding import Mesh, PartitionSpec as P

COEFF = math.sqrt(2.0 / math.pi)
AXES = ("y", "zl", "c", "zh", "x")
SIZES = (4, 8, 2, 4, 4)
F32, BF16 = jnp.float32, jnp.bfloat16
SMEM = pl.BlockSpec(memory_space=pltpu.SMEM)
VMEM = pl.BlockSpec(memory_space=pltpu.VMEM)
LATER = pl.BlockSpec(memory_space=pl.ANY)
HBM = pl.BlockSpec(memory_space=pltpu.HBM)


def gelu_value(values):
    inner = COEFF * (values + 0.044715 * values * values * values)
    return 0.5 * values * (1.0 + jnp.tanh(inner))


def gelu_slope(values):
    tangent = jnp.tanh(COEFF * (values + 0.044715 * values * values * values))
    return 0.5 * (1.0 + tangent) + 0.5 * values * (1.0 - tangent * tangent) * COEFF * (
        1.0 + 3.0 * 0.044715 * values * values
    )


def swap(value, axis, distance):
    size = lax.axis_size(axis)
    return lax.ppermute(value, axis, [(i, i ^ distance) for i in range(size)])


def shift(value, axis, distance):
    size = lax.axis_size(axis)
    return lax.ppermute(value, axis, [(i, (i + distance) % size) for i in range(size)])


def shift_both(value, distance):
    size = lax.axis_size("zh")
    pairs = [
        (core * size + i, core * size + (i + distance * (1 - 2 * core)) % size)
        for core in range(2)
        for i in range(size)
    ]
    return lax.ppermute(value, ("c", "zh"), pairs)


def dot(left, right, over_left, over_right):
    dims = (((over_left,), (over_right,)), ((), ()))
    return lax.dot_general(left, right, dims, preferred_element_type=F32)


def call(body, outs, specs, args, flops=0, scratch=(), out_specs=None, limit=14):
    moved = sum(a.size * a.dtype.itemsize for a in args) + sum(a.size for a in args)
    return pl.pallas_call(
        body,
        out_shape=[s if isinstance(s, pl.MemoryRef) else jax.ShapeDtypeStruct(*s) for s in outs],
        in_specs=specs,
        out_specs=out_specs or [VMEM] * len(outs),
        scratch_shapes=list(scratch),
        compiler_params=pltpu.CompilerParams(vmem_limit_bytes=limit << 20),
        cost_estimate=pl.CostEstimate(flops=flops, bytes_accessed=moved, transcendentals=0),
    )(*args)


def sort_channels(place, base, cot, pre, send, mine, *, block):
    core, stripe = place[0], base.shape[0]
    lanes = lax.broadcasted_iota(jnp.int32, (stripe, 2 * stripe), 1)
    own = jnp.where(lanes == base[...] + core * block, 1.0, 0.0).astype(BF16)
    other = jnp.where(lanes == base[...] + (1 - core) * block, 1.0, 0.0).astype(BF16)
    for index in range(cot.shape[1] // (2 * stripe)):
        part = cot[:, index * 2 * stripe : (index + 1) * 2 * stripe]
        rows = slice(index * stripe, (index + 1) * stripe)
        send[rows, :] = dot(other, part, 1, 1).astype(BF16)
        mine[rows, :] = dot(own, part, 1, 1).astype(BF16)
    send[mine.shape[0] :, :] = pre[...]


def weight_term(place, pre, mine, got, hidden, t0, t1, t2, t3, both, held, sems, *, stripe):
    y, tokens, channels = place[1], pre.shape[1], mine.shape[0]
    copies = [
        pltpu.make_async_copy(mine, both.at[0], sems.at[0]),
        pltpu.make_async_copy(got.at[pl.ds(0, channels)], both.at[1], sems.at[1]),
    ]
    for copy in copies:
        copy.start()
    hidden[:, :tokens] = gelu_value(pre[...].astype(F32)).astype(BF16)
    hidden[:, tokens:] = gelu_value(got[channels:, :].astype(F32)).astype(BF16)
    for index, term in enumerate((t0, t1, t2, t3)):
        rows = pl.ds(pl.multiple_of((y + index) % 4 * stripe, 16), stripe)
        total = dot(mine[rows, :], hidden[:, :tokens], 1, 1)
        total += dot(got[rows, :], hidden[:, tokens:], 1, 1)
        held[index] = total.astype(BF16)
        copies.append(pltpu.make_async_copy(held.at[index], term, sems.at[2 + index]))
        copies[-1].start()
    for copy in copies:
        copy.wait()


def split_y(place, p0, p1, p2, p3, after, keep, send):
    bit = place[2] % 2

    def total(index):
        value = p0[index].astype(F32) + p1[index].astype(F32)
        return value + (p2[index].astype(F32) + p3[index].astype(F32))

    for index in range(keep.shape[0]):
        keep[index] = total(2 * index + bit)
        send[index] = total(2 * index + 1 - bit).astype(BF16)


def split_zl(place, kept, got, keep, send, *, width):
    bit = place[2] // width % 2
    for index in range(keep.shape[0]):
        near, far = 2 * index + bit, 2 * index + 1 - bit
        keep[index] = kept[near] + got[near].astype(F32)
        send[index] = (kept[far] + got[far].astype(F32)).astype(BF16)


def sum_scaled(kept, got, out, *, factor):
    out[...] = (kept[0] + got[0].astype(F32)) * factor


def output_terms(place, w0, w1, w2, w3, hidden, out, weight, held, sems):
    core, y, zh = place[0], place[1], place[3]
    group = out.shape[2]
    pieces = (w0, w1, w2, w3)
    copies = [pltpu.make_async_copy(p, weight.at[k], sems.at[k]) for k, p in enumerate(pieces)]
    for copy in copies:
        copy.start()
    for k, piece in enumerate(pieces):
        total = dot(piece[...], hidden[...], 1, 0).astype(BF16)
        target = (y + k - zh + 4) * (1 + 2 * core) % 4
        for x in range(out.shape[0]):
            held[k, x] = total[x * group : (x + 1) * group]
        copies.append(pltpu.make_async_copy(held.at[k], out.at[:, target], sems.at[4 + k]))
        copies[-1].start()
    for copy in copies:
        copy.wait()


def sum_x(parts, after, s0, s1, s2, s3):
    for index, out in enumerate((s0, s1, s2, s3)):
        value = parts[0, index].astype(F32) + parts[1, index].astype(F32)
        value += parts[2, index].astype(F32) + parts[3, index].astype(F32)
        out[...] = value.astype(BF16)


def sum_step(s1, got, after, t1):
    t1[...] = (s1[...].astype(F32) + got[...].astype(F32)).astype(BF16)


def sum_last(s0, u, v, after, then, kept, given):
    half = kept.shape[1]
    total = (s0[...].astype(F32) + (u[...].astype(F32) + v[...].astype(F32))).astype(BF16)
    kept[...] = total[:, :half]
    given[...] = total[:, half:]


def hidden_grad(pre, own, other, out):
    out[...] = ((own[...] + other[...]) * gelu_slope(pre[...].astype(F32))).astype(BF16)


def gate(value, after, out):
    pass


def hold(value, after, place=LATER):
    return pl.pallas_call(
        gate,
        out_shape=pltpu.HBM(value.shape, value.dtype),
        in_specs=[HBM, place],
        out_specs=HBM,
        input_output_aliases={0: 0},
        compiler_params=pltpu.CompilerParams(vmem_limit_bytes=14 << 20),
    )(value, after)


def interleave(place, kept, given, out):
    core = place[0]
    for index in range(kept.shape[0]):
        out[index, core] = kept[index]
        out[index, 1 - core] = given[index]


def hidden_terms(place, weight, both, own, other):
    y, count, stripe = place[1], weight.shape[0], weight.shape[1]
    own[...] = jnp.zeros_like(own)
    other[...] = jnp.zeros_like(other)
    for k in range(count):
        rows = pl.ds(pl.multiple_of((y + k) % count * stripe, 16), stripe)
        own[...] += dot(weight[k], both[0, rows, :], 0, 0)
        other[...] += dot(weight[k], both[1, rows, :], 0, 0)


def local(base, pre_act, weight_out, cotangent):
    n_y, n_zl, n_x = SIZES[0], SIZES[1], SIZES[4]
    tokens, hid = pre_act.shape
    block = weight_out.shape[0]
    stripe = n_zl * block
    group = stripe // n_x
    channels = n_y * stripe
    place = jnp.stack([lax.axis_index(a) for a in ("c", "y", "zl", "zh", "x")]).astype(jnp.int32)
    factor = 1.0 / math.sqrt(tokens * n_y * n_zl * 2)
    work = 2 * tokens * channels * hid * 2
    pre = pre_act.T

    rows = lax.all_to_all(jnp.broadcast_to(weight_out[None], (n_zl, block, hid)), "zl", 0, 0)
    send, mine = call(
        functools.partial(sort_channels, block=block),
        [((channels + hid, tokens), BF16), ((channels, tokens), BF16)],
        [SMEM, VMEM, VMEM, VMEM],
        (place, base, cotangent, pre),
        flops=2 * 4 * tokens * stripe * stripe * 2 * 2,
        limit=56,
    )
    got = swap(send, "c", 1)
    hidden, t0, t1, t2, t3, both = call(
        functools.partial(weight_term, stripe=stripe),
        [((hid, 2 * tokens), BF16)]
        + [pltpu.HBM((stripe, hid), BF16)] * n_y
        + [pltpu.HBM((2, channels, tokens), BF16)],
        [SMEM] + [VMEM] * 3,
        (place, pre, mine, got),
        flops=work,
        scratch=[pltpu.VMEM((n_y, stripe, hid), BF16), pltpu.SemaphoreType.DMA((2 + n_y,))],
        out_specs=[VMEM] + [HBM] * (n_y + 1),
    )

    w0 = rows.reshape(stripe, hid)
    w1, w3, w2 = shift(w0, "y", -1), shift(w0, "y", 1), shift(w0, "y", 2)

    parts, weight = call(
        output_terms,
        [pltpu.HBM((n_x, n_y, group, 2 * tokens), BF16), pltpu.HBM((n_y, stripe, hid), BF16)],
        [SMEM] + [VMEM] * 5,
        (place, w0, w1, w2, w3, hidden),
        flops=work,
        scratch=[pltpu.VMEM((n_y, n_x, group, 2 * tokens), BF16), pltpu.SemaphoreType.DMA((2 * n_y,))],
        out_specs=[HBM, HBM],
    )
    t1, t2, t3 = (shift(hold(t, parts, HBM), "y", k) for k, t in ((1, t1), (2, t2), (3, t3)))
    parts = lax.all_to_all(parts, "x", 0, 0)

    whole, half = ((group, 2 * tokens), BF16), ((group, tokens), BF16)
    quarter = n_zl // 2
    terms = [t.reshape(n_zl, block, hid) for t in (t0, t1, t2, t3)]
    s0, s1, s2, s3 = call(sum_x, [whole] * 4, [VMEM, LATER], (parts, terms[3]))
    got2 = shift_both(s2, 1)
    keep, send = call(
        split_y,
        [((quarter, block, hid), F32), ((quarter, block, hid), BF16)],
        [SMEM] + [VMEM] * 4 + [LATER],
        (place, *terms, s0),
    )
    keep, send = call(
        functools.partial(split_zl, width=2),
        [((quarter // 2, block, hid), F32), ((quarter // 2, block, hid), BF16)],
        [SMEM, VMEM, VMEM],
        (place, keep, swap(send, "zl", 1)),
    )
    (s1,) = call(sum_step, [whole], [VMEM] * 2 + [LATER], (s1, got2, keep))
    u, v = shift_both(s1, 1), shift_both(s3, -1)
    own, other = call(
        hidden_terms,
        [((hid, tokens), F32)] * 2,
        [SMEM, VMEM, VMEM],
        (place, weight, both),
        flops=work,
    )
    keep, send = call(
        functools.partial(split_zl, width=4),
        [((quarter // 4, block, hid), F32), ((quarter // 4, block, hid), BF16)],
        [SMEM, VMEM, VMEM],
        (place, keep, swap(send, "zl", 2)),
    )
    (grad_pre,) = call(
        hidden_grad, [((hid, tokens), BF16)], [VMEM] * 3, (pre, own, swap(other, "c", 1))
    )
    kept, given = call(sum_last, [half] * 2, [VMEM] * 3 + [LATER] * 2, (s0, u, v, keep, grad_pre))
    (grad_weight,) = call(
        functools.partial(sum_scaled, factor=factor),
        [((block, hid), F32)],
        [VMEM] * 2,
        (keep, swap(send, "zl", 4)),
    )
    given = swap(given, "c", 1)
    (output,) = call(
        interleave,
        [((group // block, 2, block, tokens), BF16)],
        [SMEM, VMEM, VMEM],
        (place, kept.reshape(-1, block, tokens), given.reshape(-1, block, tokens)),
    )
    output = output.reshape(-1, tokens).T
    return (output, grad_pre.T, grad_weight)


def solution(mesh):
    fine = Mesh(np.asarray(mesh.devices).reshape(SIZES), AXES)
    dp, tensor = AXES[:3], AXES[3:]
    mapped = jax.shard_map(
        local,
        mesh=fine,
        in_specs=(P(None, None), P(dp, tensor), P(dp, tensor), P(dp, None)),
        out_specs=(P(dp, tensor), P(dp, tensor), P(dp, tensor)),
        check_vma=False,
    )

    def run(pre_act, weight_out, cotangent):
        block = weight_out.shape[0] // (SIZES[0] * SIZES[1] * SIZES[2])
        k = np.arange(SIZES[1] * block)
        base = (k // block * (2 * block) + k % block).astype(np.int32)[:, None]
        return mapped(jnp.asarray(base), pre_act, weight_out, cotangent)

    return run
```

```python
import functools
import math

import jax
import jax.numpy as jnp
import numpy as np
from jax import lax
from jax.experimental import pallas as pl
from jax.experimental.pallas import tpu as pltpu
from jax.sharding import Mesh, PartitionSpec as P

COEFF = math.sqrt(2.0 / math.pi)
AXES = ("y", "zl", "c", "zh", "x")
SIZES = (4, 8, 2, 4, 4)
F32, BF16 = jnp.float32, jnp.bfloat16
SMEM = pl.BlockSpec(memory_space=pltpu.SMEM)
VMEM = pl.BlockSpec(memory_space=pltpu.VMEM)
LATER = pl.BlockSpec(memory_space=pl.ANY)
HBM = pl.BlockSpec(memory_space=pltpu.HBM)


def gelu_value(values):
    inner = COEFF * (values + 0.044715 * values * values * values)
    return 0.5 * values * (1.0 + jnp.tanh(inner))


def gelu_slope(values):
    tangent = jnp.tanh(COEFF * (values + 0.044715 * values * values * values))
    return 0.5 * (1.0 + tangent) + 0.5 * values * (1.0 - tangent * tangent) * COEFF * (
        1.0 + 3.0 * 0.044715 * values * values
    )


def swap(value, axis, distance):
    size = lax.axis_size(axis)
    return lax.ppermute(value, axis, [(i, i ^ distance) for i in range(size)])


def shift(value, axis, distance):
    size = lax.axis_size(axis)
    return lax.ppermute(value, axis, [(i, (i + distance) % size) for i in range(size)])


def shift_both(value, distance):
    size = lax.axis_size("zh")
    pairs = [
        (core * size + i, core * size + (i + distance * (1 - 2 * core)) % size)
        for core in range(2)
        for i in range(size)
    ]
    return lax.ppermute(value, ("c", "zh"), pairs)


def dot(left, right, over_left, over_right):
    dims = (((over_left,), (over_right,)), ((), ()))
    return lax.dot_general(left, right, dims, preferred_element_type=F32)


def call(body, outs, specs, args, flops=0, scratch=(), out_specs=None, limit=14):
    moved = sum(a.size * a.dtype.itemsize for a in args) + sum(a.size for a in args)
    return pl.pallas_call(
        body,
        out_shape=[s if isinstance(s, pl.MemoryRef) else jax.ShapeDtypeStruct(*s) for s in outs],
        in_specs=specs,
        out_specs=out_specs or [VMEM] * len(outs),
        scratch_shapes=list(scratch),
        compiler_params=pltpu.CompilerParams(vmem_limit_bytes=limit << 20),
        cost_estimate=pl.CostEstimate(flops=flops, bytes_accessed=moved, transcendentals=0),
    )(*args)


def sort_channels(place, base, cot, pre, send, mine, *, block):
    core, stripe = place[0], base.shape[0]
    lanes = lax.broadcasted_iota(jnp.int32, (stripe, 2 * stripe), 1)
    own = jnp.where(lanes == base[...] + core * block, 1.0, 0.0).astype(BF16)
    other = jnp.where(lanes == base[...] + (1 - core) * block, 1.0, 0.0).astype(BF16)
    for index in range(cot.shape[1] // (2 * stripe)):
        part = cot[:, index * 2 * stripe : (index + 1) * 2 * stripe]
        rows = slice(index * stripe, (index + 1) * stripe)
        send[rows, :] = dot(other, part, 1, 1).astype(BF16)
        mine[rows, :] = dot(own, part, 1, 1).astype(BF16)
    send[mine.shape[0] :, :] = pre[...]


def weight_term(place, pre, mine, got, hidden, t0, t1, t2, t3, both, held, sems, *, stripe):
    y, tokens, channels = place[1], pre.shape[1], mine.shape[0]
    copies = [
        pltpu.make_async_copy(mine, both.at[0], sems.at[0]),
        pltpu.make_async_copy(got.at[pl.ds(0, channels)], both.at[1], sems.at[1]),
    ]
    for copy in copies:
        copy.start()
    hidden[:, :tokens] = gelu_value(pre[...].astype(F32)).astype(BF16)
    hidden[:, tokens:] = gelu_value(got[channels:, :].astype(F32)).astype(BF16)
    for index, term in enumerate((t0, t1, t2, t3)):
        rows = pl.ds(pl.multiple_of((y + index) % 4 * stripe, 16), stripe)
        total = dot(mine[rows, :], hidden[:, :tokens], 1, 1)
        total += dot(got[rows, :], hidden[:, tokens:], 1, 1)
        held[index] = total.astype(BF16)
        copies.append(pltpu.make_async_copy(held.at[index], term, sems.at[2 + index]))
        copies[-1].start()
    for copy in copies:
        copy.wait()


def sum_y(p0, p1, p2, p3, after, then, out, held, sem):
    value = p0[...].astype(F32) + p1[...].astype(F32)
    held[...] = (value + (p2[...].astype(F32) + p3[...].astype(F32))).astype(BF16)
    copy = pltpu.make_async_copy(held, out, sem)
    copy.start()
    copy.wait()


def sum_scaled(parts, out, *, factor):
    total = parts[0].astype(F32)
    for index in range(1, parts.shape[0]):
        total += parts[index].astype(F32)
    out[...] = total * factor


def output_terms(place, w0, w1, w2, w3, hidden, out, weight, token, held, sems):
    core, y, zh = place[0], place[1], place[3]
    group = out.shape[2]
    pieces = (w0, w1, w2, w3)
    token[...] = jnp.zeros_like(token)
    copies = [pltpu.make_async_copy(p, weight.at[k], sems.at[k]) for k, p in enumerate(pieces)]
    for copy in copies:
        copy.start()
    for k, piece in enumerate(pieces):
        total = dot(piece[...], hidden[...], 1, 0).astype(BF16)
        target = (y + k - zh + 4) * (1 + 2 * core) % 4
        for x in range(out.shape[0]):
            held[k, x] = total[x * group : (x + 1) * group]
        copies.append(pltpu.make_async_copy(held.at[k], out.at[:, target], sems.at[4 + k]))
        copies[-1].start()
    for copy in copies:
        copy.wait()


def sum_x(parts, after, s0, s1, s2, s3):
    for index, out in enumerate((s0, s1, s2, s3)):
        value = parts[0, index].astype(F32) + parts[1, index].astype(F32)
        value += parts[2, index].astype(F32) + parts[3, index].astype(F32)
        out[...] = value.astype(BF16)


def sum_step(s1, got, after, t1):
    t1[...] = (s1[...].astype(F32) + got[...].astype(F32)).astype(BF16)


def sum_last(s0, u, v, kept, given):
    half = kept.shape[1]
    total = (s0[...].astype(F32) + (u[...].astype(F32) + v[...].astype(F32))).astype(BF16)
    kept[...] = total[:, :half]
    given[...] = total[:, half:]


def hidden_grad(pre, own, other, out, token):
    token[...] = jnp.zeros_like(token)
    out[...] = ((own[...] + other[...]) * gelu_slope(pre[...].astype(F32))).astype(BF16)


def gate(value, after, out):
    pass


def hold(value, after, place=LATER):
    return pl.pallas_call(
        gate,
        out_shape=pltpu.HBM(value.shape, value.dtype),
        in_specs=[HBM, place],
        out_specs=HBM,
        input_output_aliases={0: 0},
        compiler_params=pltpu.CompilerParams(vmem_limit_bytes=14 << 20),
    )(value, after)


def interleave(place, kept, given, out):
    core = place[0]
    for index in range(kept.shape[0]):
        out[index, core] = kept[index]
        out[index, 1 - core] = given[index]


def hidden_terms(place, weight, both, own, other):
    y, count, stripe = place[1], weight.shape[0], weight.shape[1]
    own[...] = jnp.zeros_like(own)
    other[...] = jnp.zeros_like(other)
    for k in range(count):
        rows = pl.ds(pl.multiple_of((y + k) % count * stripe, 16), stripe)
        own[...] += dot(weight[k], both[0, rows, :], 0, 0)
        other[...] += dot(weight[k], both[1, rows, :], 0, 0)


def local(base, pre_act, weight_out, cotangent):
    n_y, n_zl, n_x = SIZES[0], SIZES[1], SIZES[4]
    tokens, hid = pre_act.shape
    block = weight_out.shape[0]
    stripe = n_zl * block
    group = stripe // n_x
    channels = n_y * stripe
    place = jnp.stack([lax.axis_index(a) for a in ("c", "y", "zl", "zh", "x")]).astype(jnp.int32)
    factor = 1.0 / math.sqrt(tokens * n_y * n_zl * 2)
    work = 2 * tokens * channels * hid * 2
    pre = pre_act.T

    rows = lax.all_to_all(jnp.broadcast_to(weight_out[None], (n_zl, block, hid)), "zl", 0, 0)
    send, mine = call(
        functools.partial(sort_channels, block=block),
        [((channels + hid, tokens), BF16), ((channels, tokens), BF16)],
        [SMEM, VMEM, VMEM, VMEM],
        (place, base, cotangent, pre),
        flops=2 * 4 * tokens * stripe * stripe * 2 * 2,
        limit=56,
    )
    got = swap(send, "c", 1)
    hidden, t0, t1, t2, t3, both = call(
        functools.partial(weight_term, stripe=stripe),
        [((hid, 2 * tokens), BF16)]
        + [pltpu.HBM((stripe, hid), BF16)] * n_y
        + [pltpu.HBM((2, channels, tokens), BF16)],
        [SMEM] + [VMEM] * 3,
        (place, pre, mine, got),
        flops=work,
        scratch=[pltpu.VMEM((n_y, stripe, hid), BF16), pltpu.SemaphoreType.DMA((2 + n_y,))],
        out_specs=[VMEM] + [HBM] * (n_y + 1),
    )

    w0 = rows.reshape(stripe, hid)
    w1, w3, w2 = shift(w0, "y", -1), shift(w0, "y", 1), shift(w0, "y", 2)

    parts, weight, token = call(
        output_terms,
        [pltpu.HBM((n_x, n_y, group, 2 * tokens), BF16), pltpu.HBM((n_y, stripe, hid), BF16), ((8, 128), F32)],
        [SMEM] + [VMEM] * 5,
        (place, w0, w1, w2, w3, hidden),
        flops=work,
        scratch=[pltpu.VMEM((n_y, n_x, group, 2 * tokens), BF16), pltpu.SemaphoreType.DMA((2 * n_y,))],
        out_specs=[HBM, HBM, VMEM],
    )
    t1, t2, t3 = (shift(hold(t, token), "y", k) for k, t in ((1, t1), (2, t2), (3, t3)))
    parts = lax.all_to_all(parts, "x", 0, 0)

    whole, half = ((group, 2 * tokens), BF16), ((group, tokens), BF16)
    terms = [t.reshape(n_zl, block, hid) for t in (t0, t1, t2, t3)]
    own, other = call(
        hidden_terms,
        [((hid, tokens), F32)] * 2,
        [SMEM, VMEM, VMEM],
        (place, weight, both),
        flops=work,
    )
    grad_pre, token = call(
        hidden_grad, [((hid, tokens), BF16), ((8, 128), F32)], [VMEM] * 3, (pre, own, swap(other, "c", 1))
    )
    s0, s1, s2, s3 = call(sum_x, [whole] * 4, [VMEM, LATER], (parts, token))
    got2, v = shift_both(s2, 1), shift_both(s3, -1)
    (term,) = call(
        sum_y,
        [pltpu.HBM((n_zl, block, hid), BF16)],
        [VMEM] * 4 + [LATER] * 2,
        (*terms, got2, v),
        scratch=[pltpu.VMEM((n_zl, block, hid), BF16), pltpu.SemaphoreType.DMA],
        out_specs=[HBM],
    )
    (t1,) = call(sum_step, [whole], [VMEM] * 2 + [LATER], (s1, got2, v))
    u = shift_both(t1, 1)
    kept, given = call(sum_last, [half] * 2, [VMEM] * 3, (s0, u, v))
    (grad_weight,) = call(
        functools.partial(sum_scaled, factor=factor),
        [((block, hid), F32)],
        [VMEM],
        (lax.all_to_all(term, "zl", 0, 0),),
    )
    given = swap(given, "c", 1)
    (output,) = call(
        interleave,
        [((group // block, 2, block, tokens), BF16)],
        [SMEM, VMEM, VMEM],
        (place, kept.reshape(-1, block, tokens), given.reshape(-1, block, tokens)),
    )
    output = output.reshape(-1, tokens).T
    return (output, grad_pre.T, grad_weight)


def solution(mesh):
    fine = Mesh(np.asarray(mesh.devices).reshape(SIZES), AXES)
    dp, tensor = AXES[:3], AXES[3:]
    mapped = jax.shard_map(
        local,
        mesh=fine,
        in_specs=(P(None, None), P(dp, tensor), P(dp, tensor), P(dp, None)),
        out_specs=(P(dp, tensor), P(dp, tensor), P(dp, tensor)),
        check_vma=False,
    )

    def run(pre_act, weight_out, cotangent):
        block = weight_out.shape[0] // (SIZES[0] * SIZES[1] * SIZES[2])
        k = np.arange(SIZES[1] * block)
        base = (k // block * (2 * block) + k % block).astype(np.int32)[:, None]
        return mapped(jnp.asarray(base), pre_act, weight_out, cotangent)

    return run
```

```python
import functools
import math

import jax
import jax.numpy as jnp
import numpy as np
from jax import lax
from jax.experimental import pallas as pl
from jax.experimental.pallas import tpu as pltpu
from jax.sharding import Mesh, PartitionSpec as P

COEFF = math.sqrt(2.0 / math.pi)
AXES = ("y", "zl", "c", "zh", "x")
SIZES = (4, 8, 2, 4, 4)
F32, BF16 = jnp.float32, jnp.bfloat16
SMEM = pl.BlockSpec(memory_space=pltpu.SMEM)
VMEM = pl.BlockSpec(memory_space=pltpu.VMEM)
LATER = pl.BlockSpec(memory_space=pl.ANY)
HBM = pl.BlockSpec(memory_space=pltpu.HBM)


def gelu_value(values):
    inner = COEFF * (values + 0.044715 * values * values * values)
    return 0.5 * values * (1.0 + jnp.tanh(inner))


def gelu_slope(values):
    tangent = jnp.tanh(COEFF * (values + 0.044715 * values * values * values))
    return 0.5 * (1.0 + tangent) + 0.5 * values * (1.0 - tangent * tangent) * COEFF * (
        1.0 + 3.0 * 0.044715 * values * values
    )


def swap(value, axis, distance):
    size = lax.axis_size(axis)
    return lax.ppermute(value, axis, [(i, i ^ distance) for i in range(size)])


def shift(value, axis, distance):
    size = lax.axis_size(axis)
    return lax.ppermute(value, axis, [(i, (i + distance) % size) for i in range(size)])


def shift_both(value, distance):
    size = lax.axis_size("zh")
    pairs = [
        (core * size + i, core * size + (i + distance * (1 - 2 * core)) % size)
        for core in range(2)
        for i in range(size)
    ]
    return lax.ppermute(value, ("c", "zh"), pairs)


def dot(left, right, over_left, over_right):
    dims = (((over_left,), (over_right,)), ((), ()))
    return lax.dot_general(left, right, dims, preferred_element_type=F32)


def call(body, outs, specs, args, flops=0, scratch=(), out_specs=None, limit=14):
    moved = sum(a.size * a.dtype.itemsize for a in args) + sum(a.size for a in args)
    return pl.pallas_call(
        body,
        out_shape=[s if isinstance(s, pl.MemoryRef) else jax.ShapeDtypeStruct(*s) for s in outs],
        in_specs=specs,
        out_specs=out_specs or [VMEM] * len(outs),
        scratch_shapes=list(scratch),
        compiler_params=pltpu.CompilerParams(vmem_limit_bytes=limit << 20),
        cost_estimate=pl.CostEstimate(flops=flops, bytes_accessed=moved, transcendentals=0),
    )(*args)


def sort_channels(place, base, cot, pre, send, mine, *, block):
    core, stripe = place[0], base.shape[0]
    lanes = lax.broadcasted_iota(jnp.int32, (stripe, 2 * stripe), 1)
    own = jnp.where(lanes == base[...] + core * block, 1.0, 0.0).astype(BF16)
    other = jnp.where(lanes == base[...] + (1 - core) * block, 1.0, 0.0).astype(BF16)
    for index in range(cot.shape[1] // (2 * stripe)):
        part = cot[:, index * 2 * stripe : (index + 1) * 2 * stripe]
        rows = slice(index * stripe, (index + 1) * stripe)
        send[rows, :] = dot(other, part, 1, 1).astype(BF16)
        mine[rows, :] = dot(own, part, 1, 1).astype(BF16)
    send[mine.shape[0] :, :] = pre[...]


def weight_term(place, pre, mine, got, hidden, t0, t1, t2, t3, both, held, sems, *, stripe):
    y, tokens, channels = place[1], pre.shape[1], mine.shape[0]
    copies = [
        pltpu.make_async_copy(mine, both.at[0], sems.at[0]),
        pltpu.make_async_copy(got.at[pl.ds(0, channels)], both.at[1], sems.at[1]),
    ]
    for copy in copies:
        copy.start()
    hidden[:, :tokens] = gelu_value(pre[...].astype(F32)).astype(BF16)
    hidden[:, tokens:] = gelu_value(got[channels:, :].astype(F32)).astype(BF16)
    for index, term in enumerate((t0, t1, t2, t3)):
        rows = pl.ds(pl.multiple_of((y + index) % 4 * stripe, 16), stripe)
        total = dot(mine[rows, :], hidden[:, :tokens], 1, 1)
        total += dot(got[rows, :], hidden[:, tokens:], 1, 1)
        held[index] = total.astype(BF16)
        copies.append(pltpu.make_async_copy(held.at[index], term, sems.at[2 + index]))
        copies[-1].start()
    for copy in copies:
        copy.wait()


def split_y(place, p0, p1, p2, p3, keep, send):
    bit = place[2] % 2

    def total(index):
        value = p0[index].astype(F32) + p1[index].astype(F32)
        return value + (p2[index].astype(F32) + p3[index].astype(F32))

    for index in range(keep.shape[0]):
        keep[index] = total(2 * index + bit)
        send[index] = total(2 * index + 1 - bit).astype(BF16)


def split_zl(place, kept, got, keep, send, *, width):
    bit = place[2] // width % 2
    for index in range(keep.shape[0]):
        near, far = 2 * index + bit, 2 * index + 1 - bit
        keep[index] = kept[near] + got[near].astype(F32)
        send[index] = (kept[far] + got[far].astype(F32)).astype(BF16)


def sum_scaled(kept, got, out, *, factor):
    out[...] = (kept[0] + got[0].astype(F32)) * factor


def output_terms(place, w0, w1, w2, w3, hidden, a0, a1, a2, out, weight, token, held, sems):
    core, y, zh = place[0], place[1], place[3]
    group = out.shape[2]
    pieces = (w0, w1, w2, w3)
    token[...] = jnp.zeros_like(token)
    copies = [pltpu.make_async_copy(p, weight.at[k], sems.at[k]) for k, p in enumerate(pieces)]
    for copy in copies:
        copy.start()
    for k, piece in enumerate(pieces):
        total = dot(piece[...], hidden[...], 1, 0).astype(BF16)
        target = (y + k - zh + 4) * (1 + 2 * core) % 4
        for x in range(out.shape[0]):
            held[k, x] = total[x * group : (x + 1) * group]
        copies.append(pltpu.make_async_copy(held.at[k], out.at[:, target], sems.at[4 + k]))
        copies[-1].start()
    for copy in copies:
        copy.wait()


def sum_x(parts, after, then, s0, s1, s2, s3):
    for index, out in enumerate((s0, s1, s2, s3)):
        value = parts[0, index].astype(F32) + parts[1, index].astype(F32)
        value += parts[2, index].astype(F32) + parts[3, index].astype(F32)
        out[...] = value.astype(BF16)


def sum_step(s1, got, after, then, t1):
    t1[...] = (s1[...].astype(F32) + got[...].astype(F32)).astype(BF16)


def sum_last(s0, u, v, kept, given):
    half = kept.shape[1]
    total = (s0[...].astype(F32) + (u[...].astype(F32) + v[...].astype(F32))).astype(BF16)
    kept[...] = total[:, :half]
    given[...] = total[:, half:]


def hidden_grad(pre, own, other, out, token):
    token[...] = jnp.zeros_like(token)
    out[...] = ((own[...] + other[...]) * gelu_slope(pre[...].astype(F32))).astype(BF16)


def interleave(place, kept, given, out):
    core = place[0]
    for index in range(kept.shape[0]):
        out[index, core] = kept[index]
        out[index, 1 - core] = given[index]


def hidden_terms(place, weight, both, own, other):
    y, count, stripe = place[1], weight.shape[0], weight.shape[1]
    own[...] = jnp.zeros_like(own)
    other[...] = jnp.zeros_like(other)
    for k in range(count):
        rows = pl.ds(pl.multiple_of((y + k) % count * stripe, 16), stripe)
        own[...] += dot(weight[k], both[0, rows, :], 0, 0)
        other[...] += dot(weight[k], both[1, rows, :], 0, 0)


def local(base, pre_act, weight_out, cotangent):
    n_y, n_zl, n_x = SIZES[0], SIZES[1], SIZES[4]
    tokens, hid = pre_act.shape
    block = weight_out.shape[0]
    stripe = n_zl * block
    group = stripe // n_x
    channels = n_y * stripe
    place = jnp.stack([lax.axis_index(a) for a in ("c", "y", "zl", "zh", "x")]).astype(jnp.int32)
    factor = 1.0 / math.sqrt(tokens * n_y * n_zl * 2)
    work = 2 * tokens * channels * hid * 2
    pre = pre_act.T

    rows = lax.all_to_all(jnp.broadcast_to(weight_out[None], (n_zl, block, hid)), "zl", 0, 0)
    send, mine = call(
        functools.partial(sort_channels, block=block),
        [((channels + hid, tokens), BF16), ((channels, tokens), BF16)],
        [SMEM, VMEM, VMEM, VMEM],
        (place, base, cotangent, pre),
        flops=2 * 4 * tokens * stripe * stripe * 2 * 2,
        limit=56,
    )
    got = swap(send, "c", 1)
    hidden, t0, t1, t2, t3, both = call(
        functools.partial(weight_term, stripe=stripe),
        [((hid, 2 * tokens), BF16)]
        + [pltpu.HBM((stripe, hid), BF16)] * n_y
        + [pltpu.HBM((2, channels, tokens), BF16)],
        [SMEM] + [VMEM] * 3,
        (place, pre, mine, got),
        flops=work,
        scratch=[pltpu.VMEM((n_y, stripe, hid), BF16), pltpu.SemaphoreType.DMA((2 + n_y,))],
        out_specs=[VMEM] + [HBM] * (n_y + 1),
    )

    w0 = rows.reshape(stripe, hid)
    w1, w3, w2 = shift(w0, "y", -1), shift(w0, "y", 1), shift(w0, "y", 2)

    t1, t2, t3 = (shift(t, "y", k) for k, t in ((1, t1), (2, t2), (3, t3)))
    parts, weight, token = call(
        output_terms,
        [pltpu.HBM((n_x, n_y, group, 2 * tokens), BF16), pltpu.HBM((n_y, stripe, hid), BF16), ((8, 128), F32)],
        [SMEM] + [VMEM] * 5 + [LATER] * 3,
        (place, w0, w1, w2, w3, hidden, t1, t3, t2),
        flops=work,
        scratch=[pltpu.VMEM((n_y, n_x, group, 2 * tokens), BF16), pltpu.SemaphoreType.DMA((2 * n_y,))],
        out_specs=[HBM, HBM, VMEM],
    )
    parts = lax.all_to_all(parts, "x", 0, 0)

    whole, half = ((group, 2 * tokens), BF16), ((group, tokens), BF16)
    terms = [t.reshape(n_zl, block, hid) for t in (t0, t1, t2, t3)]
    own, other = call(
        hidden_terms,
        [((hid, tokens), F32)] * 2,
        [SMEM, VMEM, VMEM],
        (place, weight, both),
        flops=work,
    )
    grad_pre, token = call(
        hidden_grad, [((hid, tokens), BF16), ((8, 128), F32)], [VMEM] * 3, (pre, own, swap(other, "c", 1))
    )
    quarter = n_zl // 2
    keep, send = call(
        split_y,
        [((quarter, block, hid), F32), ((quarter, block, hid), BF16)],
        [SMEM] + [VMEM] * 4,
        (place, *terms),
    )
    for width in (2, 4):
        quarter //= 2
        keep, send = call(
            functools.partial(split_zl, width=width),
            [((quarter, block, hid), F32), ((quarter, block, hid), BF16)],
            [SMEM, VMEM, VMEM],
            (place, keep, swap(send, "zl", width // 2)),
        )
    s0, s1, s2, s3 = call(sum_x, [whole] * 4, [VMEM] + [LATER] * 2, (parts, token, keep))
    got2, v = shift_both(s2, 1), shift_both(s3, -1)
    (grad_weight,) = call(
        functools.partial(sum_scaled, factor=factor),
        [((block, hid), F32)],
        [VMEM] * 2,
        (keep, swap(send, "zl", 4)),
    )
    (t1,) = call(sum_step, [whole], [VMEM] * 2 + [LATER] * 2, (s1, got2, v, grad_weight))
    u = shift_both(t1, 1)
    kept, given = call(sum_last, [half] * 2, [VMEM] * 3, (s0, u, v))
    given = swap(given, "c", 1)
    (output,) = call(
        interleave,
        [((group // block, 2, block, tokens), BF16)],
        [SMEM, VMEM, VMEM],
        (place, kept.reshape(-1, block, tokens), given.reshape(-1, block, tokens)),
    )
    output = output.reshape(-1, tokens).T
    return (output, grad_pre.T, grad_weight)


def solution(mesh):
    fine = Mesh(np.asarray(mesh.devices).reshape(SIZES), AXES)
    dp, tensor = AXES[:3], AXES[3:]
    mapped = jax.shard_map(
        local,
        mesh=fine,
        in_specs=(P(None, None), P(dp, tensor), P(dp, tensor), P(dp, None)),
        out_specs=(P(dp, tensor), P(dp, tensor), P(dp, tensor)),
        check_vma=False,
    )

    def run(pre_act, weight_out, cotangent):
        block = weight_out.shape[0] // (SIZES[0] * SIZES[1] * SIZES[2])
        k = np.arange(SIZES[1] * block)
        base = (k // block * (2 * block) + k % block).astype(np.int32)[:, None]
        return mapped(jnp.asarray(base), pre_act, weight_out, cotangent)

    return run
```

```python
import functools
import math

import jax
import jax.numpy as jnp
import numpy as np
from jax import lax
from jax.experimental import pallas as pl
from jax.experimental.pallas import tpu as pltpu
from jax.sharding import Mesh, PartitionSpec as P

COEFF = math.sqrt(2.0 / math.pi)
AXES = ("y", "zl", "c", "zh", "x")
SIZES = (4, 8, 2, 4, 4)
F32, BF16 = jnp.float32, jnp.bfloat16
SMEM = pl.BlockSpec(memory_space=pltpu.SMEM)
VMEM = pl.BlockSpec(memory_space=pltpu.VMEM)
LATER = pl.BlockSpec(memory_space=pl.ANY)
HBM = pl.BlockSpec(memory_space=pltpu.HBM)


def gelu_value(values):
    inner = COEFF * (values + 0.044715 * values * values * values)
    return 0.5 * values * (1.0 + jnp.tanh(inner))


def gelu_slope(values):
    tangent = jnp.tanh(COEFF * (values + 0.044715 * values * values * values))
    return 0.5 * (1.0 + tangent) + 0.5 * values * (1.0 - tangent * tangent) * COEFF * (
        1.0 + 3.0 * 0.044715 * values * values
    )


def swap(value, axis, distance):
    size = lax.axis_size(axis)
    return lax.ppermute(value, axis, [(i, i ^ distance) for i in range(size)])


def shift(value, axis, distance):
    size = lax.axis_size(axis)
    return lax.ppermute(value, axis, [(i, (i + distance) % size) for i in range(size)])


def shift_both(value, distance):
    size = lax.axis_size("zh")
    pairs = [
        (core * size + i, core * size + (i + distance * (1 - 2 * core)) % size)
        for core in range(2)
        for i in range(size)
    ]
    return lax.ppermute(value, ("c", "zh"), pairs)


def dot(left, right, over_left, over_right):
    dims = (((over_left,), (over_right,)), ((), ()))
    return lax.dot_general(left, right, dims, preferred_element_type=F32)


def call(body, outs, specs, args, flops=0, scratch=(), out_specs=None, limit=14):
    moved = sum(a.size * a.dtype.itemsize for a in args) + sum(a.size for a in args)
    return pl.pallas_call(
        body,
        out_shape=[s if isinstance(s, pl.MemoryRef) else jax.ShapeDtypeStruct(*s) for s in outs],
        in_specs=specs,
        out_specs=out_specs or [VMEM] * len(outs),
        scratch_shapes=list(scratch),
        compiler_params=pltpu.CompilerParams(vmem_limit_bytes=limit << 20),
        cost_estimate=pl.CostEstimate(flops=flops, bytes_accessed=moved, transcendentals=0),
    )(*args)


def sort_channels(place, base, cot, pre, send, mine, *, block):
    core, stripe = place[0], base.shape[0]
    lanes = lax.broadcasted_iota(jnp.int32, (stripe, 2 * stripe), 1)
    own = jnp.where(lanes == base[...] + core * block, 1.0, 0.0).astype(BF16)
    other = jnp.where(lanes == base[...] + (1 - core) * block, 1.0, 0.0).astype(BF16)
    for index in range(cot.shape[1] // (2 * stripe)):
        part = cot[:, index * 2 * stripe : (index + 1) * 2 * stripe]
        rows = slice(index * stripe, (index + 1) * stripe)
        send[rows, :] = dot(other, part, 1, 1).astype(BF16)
        mine[rows, :] = dot(own, part, 1, 1).astype(BF16)
    send[mine.shape[0] :, :] = pre[...]


def weight_term(place, pre, mine, got, hidden, t0, t1, t2, t3, both, held, sems, *, stripe):
    y, tokens, channels = place[1], pre.shape[1], mine.shape[0]
    copies = [
        pltpu.make_async_copy(mine, both.at[0], sems.at[0]),
        pltpu.make_async_copy(got.at[pl.ds(0, channels)], both.at[1], sems.at[1]),
    ]
    for copy in copies:
        copy.start()
    hidden[:, :tokens] = gelu_value(pre[...].astype(F32)).astype(BF16)
    hidden[:, tokens:] = gelu_value(got[channels:, :].astype(F32)).astype(BF16)
    for index, term in enumerate((t0, t1, t2, t3)):
        rows = pl.ds(pl.multiple_of((y + index) % 4 * stripe, 16), stripe)
        total = dot(mine[rows, :], hidden[:, :tokens], 1, 1)
        total += dot(got[rows, :], hidden[:, tokens:], 1, 1)
        held[index] = total.astype(BF16)
        copies.append(pltpu.make_async_copy(held.at[index], term, sems.at[2 + index]))
        copies[-1].start()
    for copy in copies:
        copy.wait()


def split_y(place, p0, p1, p2, p3, after, then, keep, send):
    bit = place[2] % 2

    def total(index):
        value = p0[index].astype(F32) + p1[index].astype(F32)
        return value + (p2[index].astype(F32) + p3[index].astype(F32))

    for index in range(keep.shape[0]):
        keep[index] = total(2 * index + bit)
        send[index] = total(2 * index + 1 - bit).astype(BF16)


def split_pairs(place, kept, got, own, q1, q2, q3):
    pair = place[2] // 2
    own[...] = kept[pair] + got[pair].astype(F32)
    for index, out in enumerate((q1, q2, q3)):
        block = pair ^ (index + 1)
        out[...] = (kept[block] + got[block].astype(F32)).astype(BF16)


def sum_scaled(own, r1, r2, r3, out, *, factor):
    total = own[...] + r1[...].astype(F32)
    out[...] = (total + (r2[...].astype(F32) + r3[...].astype(F32))) * factor


def output_terms(place, w0, w1, w2, w3, hidden, out, weight, token, held, sems):
    core, y, zh = place[0], place[1], place[3]
    group = out.shape[2]
    pieces = (w0, w1, w2, w3)
    token[...] = jnp.zeros_like(token)
    copies = [pltpu.make_async_copy(p, weight.at[k], sems.at[k]) for k, p in enumerate(pieces)]
    for copy in copies:
        copy.start()
    for k, piece in enumerate(pieces):
        total = dot(piece[...], hidden[...], 1, 0).astype(BF16)
        target = (y + k - zh + 4) * (1 + 2 * core) % 4
        for x in range(out.shape[0]):
            held[k, x] = total[x * group : (x + 1) * group]
        copies.append(pltpu.make_async_copy(held.at[k], out.at[:, target], sems.at[4 + k]))
        copies[-1].start()
    for copy in copies:
        copy.wait()


def sum_x(parts, after, s0, s1, s2, s3):
    for index, out in enumerate((s0, s1, s2, s3)):
        value = parts[0, index].astype(F32) + parts[1, index].astype(F32)
        value += parts[2, index].astype(F32) + parts[3, index].astype(F32)
        out[...] = value.astype(BF16)


def sum_step(s1, got, after, t1):
    t1[...] = (s1[...].astype(F32) + got[...].astype(F32)).astype(BF16)


def sum_last(s0, u, v, r1, r2, r3, kept, given):
    half = kept.shape[1]
    total = (s0[...].astype(F32) + (u[...].astype(F32) + v[...].astype(F32))).astype(BF16)
    kept[...] = total[:, :half]
    given[...] = total[:, half:]


def hidden_grad(pre, own, other, out, token):
    token[...] = jnp.zeros_like(token)
    out[...] = ((own[...] + other[...]) * gelu_slope(pre[...].astype(F32))).astype(BF16)


def gate(value, after, out):
    pass


def hold(value, after, place=LATER):
    return pl.pallas_call(
        gate,
        out_shape=pltpu.HBM(value.shape, value.dtype),
        in_specs=[HBM, place],
        out_specs=HBM,
        input_output_aliases={0: 0},
        compiler_params=pltpu.CompilerParams(vmem_limit_bytes=14 << 20),
    )(value, after)


def interleave(place, kept, given, out):
    core = place[0]
    for index in range(kept.shape[0]):
        out[index, core] = kept[index]
        out[index, 1 - core] = given[index]


def hidden_terms(place, weight, both, own, other):
    y, count, stripe = place[1], weight.shape[0], weight.shape[1]
    own[...] = jnp.zeros_like(own)
    other[...] = jnp.zeros_like(other)
    for k in range(count):
        rows = pl.ds(pl.multiple_of((y + k) % count * stripe, 16), stripe)
        own[...] += dot(weight[k], both[0, rows, :], 0, 0)
        other[...] += dot(weight[k], both[1, rows, :], 0, 0)


def local(base, pre_act, weight_out, cotangent):
    n_y, n_zl, n_x = SIZES[0], SIZES[1], SIZES[4]
    tokens, hid = pre_act.shape
    block = weight_out.shape[0]
    stripe = n_zl * block
    group = stripe // n_x
    channels = n_y * stripe
    place = jnp.stack([lax.axis_index(a) for a in ("c", "y", "zl", "zh", "x")]).astype(jnp.int32)
    factor = 1.0 / math.sqrt(tokens * n_y * n_zl * 2)
    work = 2 * tokens * channels * hid * 2
    pre = pre_act.T

    rows = lax.all_to_all(jnp.broadcast_to(weight_out[None], (n_zl, block, hid)), "zl", 0, 0)
    send, mine = call(
        functools.partial(sort_channels, block=block),
        [((channels + hid, tokens), BF16), ((channels, tokens), BF16)],
        [SMEM, VMEM, VMEM, VMEM],
        (place, base, cotangent, pre),
        flops=2 * 4 * tokens * stripe * stripe * 2 * 2,
        limit=56,
    )
    got = swap(send, "c", 1)
    hidden, t0, t1, t2, t3, both = call(
        functools.partial(weight_term, stripe=stripe),
        [((hid, 2 * tokens), BF16)]
        + [pltpu.HBM((stripe, hid), BF16)] * n_y
        + [pltpu.HBM((2, channels, tokens), BF16)],
        [SMEM] + [VMEM] * 3,
        (place, pre, mine, got),
        flops=work,
        scratch=[pltpu.VMEM((n_y, stripe, hid), BF16), pltpu.SemaphoreType.DMA((2 + n_y,))],
        out_specs=[VMEM] + [HBM] * (n_y + 1),
    )

    w0 = rows.reshape(stripe, hid)
    w1, w3, w2 = shift(w0, "y", -1), shift(w0, "y", 1), shift(w0, "y", 2)

    parts, weight, token = call(
        output_terms,
        [pltpu.HBM((n_x, n_y, group, 2 * tokens), BF16), pltpu.HBM((n_y, stripe, hid), BF16), ((8, 128), F32)],
        [SMEM] + [VMEM] * 5,
        (place, w0, w1, w2, w3, hidden),
        flops=work,
        scratch=[pltpu.VMEM((n_y, n_x, group, 2 * tokens), BF16), pltpu.SemaphoreType.DMA((2 * n_y,))],
        out_specs=[HBM, HBM, VMEM],
    )
    t1, t2, t3 = (shift(hold(t, token), "y", k) for k, t in ((1, t1), (2, t2), (3, t3)))
    parts = lax.all_to_all(parts, "x", 0, 0)

    whole, half = ((group, 2 * tokens), BF16), ((group, tokens), BF16)
    terms = [t.reshape(n_zl, block, hid) for t in (t0, t1, t2, t3)]
    own, other = call(
        hidden_terms,
        [((hid, tokens), F32)] * 2,
        [SMEM, VMEM, VMEM],
        (place, weight, both),
        flops=work,
    )
    grad_pre, token = call(
        hidden_grad, [((hid, tokens), BF16), ((8, 128), F32)], [VMEM] * 3, (pre, own, swap(other, "c", 1))
    )
    s0, s1, s2, s3 = call(sum_x, [whole] * 4, [VMEM, LATER], (parts, token))
    got2, v = shift_both(s2, 1), shift_both(s3, -1)
    quarter = n_zl // 2
    keep, send = call(
        split_y,
        [((quarter, block, hid), F32), ((quarter, block, hid), BF16)],
        [SMEM] + [VMEM] * 4 + [LATER] * 2,
        (place, *terms, got2, v),
    )
    (t1,) = call(sum_step, [whole], [VMEM] * 2 + [LATER], (s1, got2, v))
    u = shift_both(t1, 1)
    partial, *pairs = call(
        split_pairs,
        [((block, hid), F32)] + [((block, hid), BF16)] * 3,
        [SMEM, VMEM, VMEM],
        (place, keep, swap(send, "zl", 1)),
    )
    pairs = [swap(p, "zl", 2 * (k + 1)) for k, p in enumerate(pairs)]
    kept, given = call(sum_last, [half] * 2, [VMEM] * 3 + [LATER] * 3, (s0, u, v, *pairs))
    (grad_weight,) = call(
        functools.partial(sum_scaled, factor=factor),
        [((block, hid), F32)],
        [VMEM] * 4,
        (partial, *pairs),
    )
    given = swap(given, "c", 1)
    (output,) = call(
        interleave,
        [((group // block, 2, block, tokens), BF16)],
        [SMEM, VMEM, VMEM],
        (place, kept.reshape(-1, block, tokens), given.reshape(-1, block, tokens)),
    )
    output = output.reshape(-1, tokens).T
    return (output, grad_pre.T, grad_weight)


def solution(mesh):
    fine = Mesh(np.asarray(mesh.devices).reshape(SIZES), AXES)
    dp, tensor = AXES[:3], AXES[3:]
    mapped = jax.shard_map(
        local,
        mesh=fine,
        in_specs=(P(None, None), P(dp, tensor), P(dp, tensor), P(dp, None)),
        out_specs=(P(dp, tensor), P(dp, tensor), P(dp, tensor)),
        check_vma=False,
    )

    def run(pre_act, weight_out, cotangent):
        block = weight_out.shape[0] // (SIZES[0] * SIZES[1] * SIZES[2])
        k = np.arange(SIZES[1] * block)
        base = (k // block * (2 * block) + k % block).astype(np.int32)[:, None]
        return mapped(jnp.asarray(base), pre_act, weight_out, cotangent)

    return run
```

```python
import functools
import math

import jax
import jax.numpy as jnp
import numpy as np
from jax import lax
from jax.experimental import pallas as pl
from jax.experimental.pallas import tpu as pltpu
from jax.sharding import Mesh, PartitionSpec as P

COEFF = math.sqrt(2.0 / math.pi)
AXES = ("y", "zl", "c", "zh", "x")
SIZES = (4, 8, 2, 4, 4)
F32, BF16 = jnp.float32, jnp.bfloat16
SMEM = pl.BlockSpec(memory_space=pltpu.SMEM)
VMEM = pl.BlockSpec(memory_space=pltpu.VMEM)
LATER = pl.BlockSpec(memory_space=pl.ANY)
HBM = pl.BlockSpec(memory_space=pltpu.HBM)


def gelu_value(values):
    inner = COEFF * (values + 0.044715 * values * values * values)
    return 0.5 * values * (1.0 + jnp.tanh(inner))


def gelu_slope(values):
    tangent = jnp.tanh(COEFF * (values + 0.044715 * values * values * values))
    return 0.5 * (1.0 + tangent) + 0.5 * values * (1.0 - tangent * tangent) * COEFF * (
        1.0 + 3.0 * 0.044715 * values * values
    )


def swap(value, axis, distance):
    size = lax.axis_size(axis)
    return lax.ppermute(value, axis, [(i, i ^ distance) for i in range(size)])


def shift(value, axis, distance):
    size = lax.axis_size(axis)
    return lax.ppermute(value, axis, [(i, (i + distance) % size) for i in range(size)])


def shift_both(value, distance):
    size = lax.axis_size("zh")
    pairs = [
        (core * size + i, core * size + (i + distance * (1 - 2 * core)) % size)
        for core in range(2)
        for i in range(size)
    ]
    return lax.ppermute(value, ("c", "zh"), pairs)


def dot(left, right, over_left, over_right):
    dims = (((over_left,), (over_right,)), ((), ()))
    return lax.dot_general(left, right, dims, preferred_element_type=F32)


def call(body, outs, specs, args, flops=0, scratch=(), out_specs=None, limit=14):
    moved = sum(a.size * a.dtype.itemsize for a in args) + sum(a.size for a in args)
    return pl.pallas_call(
        body,
        out_shape=[s if isinstance(s, pl.MemoryRef) else jax.ShapeDtypeStruct(*s) for s in outs],
        in_specs=specs,
        out_specs=out_specs or [VMEM] * len(outs),
        scratch_shapes=list(scratch),
        compiler_params=pltpu.CompilerParams(vmem_limit_bytes=limit << 20),
        cost_estimate=pl.CostEstimate(flops=flops, bytes_accessed=moved, transcendentals=0),
    )(*args)


def sort_channels(place, base, cot, pre, send, mine, *, block):
    core, stripe = place[0], base.shape[0]
    lanes = lax.broadcasted_iota(jnp.int32, (stripe, 2 * stripe), 1)
    own = jnp.where(lanes == base[...] + core * block, 1.0, 0.0).astype(BF16)
    other = jnp.where(lanes == base[...] + (1 - core) * block, 1.0, 0.0).astype(BF16)
    for index in range(cot.shape[1] // (2 * stripe)):
        part = cot[:, index * 2 * stripe : (index + 1) * 2 * stripe]
        rows = slice(index * stripe, (index + 1) * stripe)
        send[rows, :] = dot(other, part, 1, 1).astype(BF16)
        mine[rows, :] = dot(own, part, 1, 1).astype(BF16)
    send[mine.shape[0] :, :] = pre[...]


def weight_term(place, pre, mine, got, hidden, t0, t1, t2, t3, both, held, sems, *, stripe):
    y, tokens, channels = place[1], pre.shape[1], mine.shape[0]
    copies = [
        pltpu.make_async_copy(mine, both.at[0], sems.at[0]),
        pltpu.make_async_copy(got.at[pl.ds(0, channels)], both.at[1], sems.at[1]),
    ]
    for copy in copies:
        copy.start()
    hidden[:, :tokens] = gelu_value(pre[...].astype(F32)).astype(BF16)
    hidden[:, tokens:] = gelu_value(got[channels:, :].astype(F32)).astype(BF16)
    for index, term in enumerate((t0, t1, t2, t3)):
        rows = pl.ds(pl.multiple_of((y + index) % 4 * stripe, 16), stripe)
        total = dot(mine[rows, :], hidden[:, :tokens], 1, 1)
        total += dot(got[rows, :], hidden[:, tokens:], 1, 1)
        held[index] = total.astype(BF16)
        copies.append(pltpu.make_async_copy(held.at[index], term, sems.at[2 + index]))
        copies[-1].start()
    for copy in copies:
        copy.wait()


def split_y(place, p0, p1, p2, p3, after, then, keep, send):
    bit = place[2] % 2

    def total(index):
        value = p0[index].astype(F32) + p1[index].astype(F32)
        return value + (p2[index].astype(F32) + p3[index].astype(F32))

    for index in range(keep.shape[0]):
        keep[index] = total(2 * index + bit)
        send[index] = total(2 * index + 1 - bit).astype(BF16)


def split_pairs(place, kept, got, own, q1, q2, q3):
    pair = place[2] // 2
    own[...] = kept[pair] + got[pair].astype(F32)
    for index, out in enumerate((q1, q2, q3)):
        block = pair ^ (index + 1)
        out[...] = (kept[block] + got[block].astype(F32)).astype(BF16)


def sum_scaled(own, r1, r2, r3, out, *, factor):
    total = own[...] + r1[...].astype(F32)
    out[...] = (total + (r2[...].astype(F32) + r3[...].astype(F32))) * factor


def output_terms(place, w0, w1, w2, w3, hidden, out, weight, token, held, sems):
    core, y, zh = place[0], place[1], place[3]
    group = out.shape[2]
    pieces = (w0, w1, w2, w3)
    token[...] = jnp.zeros_like(token)
    copies = [pltpu.make_async_copy(p, weight.at[k], sems.at[k]) for k, p in enumerate(pieces)]
    for copy in copies:
        copy.start()
    for k, piece in enumerate(pieces):
        total = dot(piece[...], hidden[...], 1, 0).astype(BF16)
        target = (y + k - zh + 4) * (1 + 2 * core) % 4
        for x in range(out.shape[0]):
            held[k, x] = total[x * group : (x + 1) * group]
        copies.append(pltpu.make_async_copy(held.at[k], out.at[:, target], sems.at[4 + k]))
        copies[-1].start()
    for copy in copies:
        copy.wait()


def sum_x(parts, after, s0, s1, s2, s3):
    for index, out in enumerate((s0, s1, s2, s3)):
        value = parts[0, index].astype(F32) + parts[1, index].astype(F32)
        value += parts[2, index].astype(F32) + parts[3, index].astype(F32)
        out[...] = value.astype(BF16)


def sum_step(s1, got, after, t1):
    t1[...] = (s1[...].astype(F32) + got[...].astype(F32)).astype(BF16)


def sum_last(s0, u, v, r1, r2, kept, given):
    half = kept.shape[1]
    total = (s0[...].astype(F32) + (u[...].astype(F32) + v[...].astype(F32))).astype(BF16)
    kept[...] = total[:, :half]
    given[...] = total[:, half:]


def hidden_grad(pre, own, other, out, token):
    token[...] = jnp.zeros_like(token)
    out[...] = ((own[...] + other[...]) * gelu_slope(pre[...].astype(F32))).astype(BF16)


def gate(value, after, out):
    pass


def hold(value, after, place=LATER):
    return pl.pallas_call(
        gate,
        out_shape=pltpu.HBM(value.shape, value.dtype),
        in_specs=[HBM, place],
        out_specs=HBM,
        input_output_aliases={0: 0},
        compiler_params=pltpu.CompilerParams(vmem_limit_bytes=14 << 20),
    )(value, after)


def interleave(place, kept, given, out):
    core = place[0]
    for index in range(kept.shape[0]):
        out[index, core] = kept[index]
        out[index, 1 - core] = given[index]


def hidden_terms(place, weight, both, own, other):
    y, count, stripe = place[1], weight.shape[0], weight.shape[1]
    own[...] = jnp.zeros_like(own)
    other[...] = jnp.zeros_like(other)
    for k in range(count):
        rows = pl.ds(pl.multiple_of((y + k) % count * stripe, 16), stripe)
        own[...] += dot(weight[k], both[0, rows, :], 0, 0)
        other[...] += dot(weight[k], both[1, rows, :], 0, 0)


def local(base, pre_act, weight_out, cotangent):
    n_y, n_zl, n_x = SIZES[0], SIZES[1], SIZES[4]
    tokens, hid = pre_act.shape
    block = weight_out.shape[0]
    stripe = n_zl * block
    group = stripe // n_x
    channels = n_y * stripe
    place = jnp.stack([lax.axis_index(a) for a in ("c", "y", "zl", "zh", "x")]).astype(jnp.int32)
    factor = 1.0 / math.sqrt(tokens * n_y * n_zl * 2)
    work = 2 * tokens * channels * hid * 2
    pre = pre_act.T

    rows = lax.all_to_all(jnp.broadcast_to(weight_out[None], (n_zl, block, hid)), "zl", 0, 0)
    send, mine = call(
        functools.partial(sort_channels, block=block),
        [((channels + hid, tokens), BF16), ((channels, tokens), BF16)],
        [SMEM, VMEM, VMEM, VMEM],
        (place, base, cotangent, pre),
        flops=2 * 4 * tokens * stripe * stripe * 2 * 2,
        limit=56,
    )
    got = swap(send, "c", 1)
    hidden, t0, t1, t2, t3, both = call(
        functools.partial(weight_term, stripe=stripe),
        [((hid, 2 * tokens), BF16)]
        + [pltpu.HBM((stripe, hid), BF16)] * n_y
        + [pltpu.HBM((2, channels, tokens), BF16)],
        [SMEM] + [VMEM] * 3,
        (place, pre, mine, got),
        flops=work,
        scratch=[pltpu.VMEM((n_y, stripe, hid), BF16), pltpu.SemaphoreType.DMA((2 + n_y,))],
        out_specs=[VMEM] + [HBM] * (n_y + 1),
    )

    w0 = rows.reshape(stripe, hid)
    w1, w3, w2 = shift(w0, "y", -1), shift(w0, "y", 1), shift(w0, "y", 2)

    parts, weight, token = call(
        output_terms,
        [pltpu.HBM((n_x, n_y, group, 2 * tokens), BF16), pltpu.HBM((n_y, stripe, hid), BF16), ((8, 128), F32)],
        [SMEM] + [VMEM] * 5,
        (place, w0, w1, w2, w3, hidden),
        flops=work,
        scratch=[pltpu.VMEM((n_y, n_x, group, 2 * tokens), BF16), pltpu.SemaphoreType.DMA((2 * n_y,))],
        out_specs=[HBM, HBM, VMEM],
    )
    t1, t2, t3 = (shift(hold(t, token), "y", k) for k, t in ((1, t1), (2, t2), (3, t3)))
    parts = lax.all_to_all(parts, "x", 0, 0)

    whole, half = ((group, 2 * tokens), BF16), ((group, tokens), BF16)
    terms = [t.reshape(n_zl, block, hid) for t in (t0, t1, t2, t3)]
    own, other = call(
        hidden_terms,
        [((hid, tokens), F32)] * 2,
        [SMEM, VMEM, VMEM],
        (place, weight, both),
        flops=work,
        limit=56,
    )
    grad_pre, token = call(
        hidden_grad, [((hid, tokens), BF16), ((8, 128), F32)], [VMEM] * 3, (pre, own, swap(other, "c", 1))
    )
    s0, s1, s2, s3 = call(sum_x, [whole] * 4, [VMEM, LATER], (parts, token))
    got2, v = shift_both(s2, 1), shift_both(s3, -1)
    quarter = n_zl // 2
    keep, send = call(
        split_y,
        [((quarter, block, hid), F32), ((quarter, block, hid), BF16)],
        [SMEM] + [VMEM] * 4 + [LATER] * 2,
        (place, *terms, got2, v),
    )
    (t1,) = call(sum_step, [whole], [VMEM] * 2 + [LATER], (s1, got2, v))
    u = shift_both(t1, 1)
    partial, *pairs = call(
        split_pairs,
        [((block, hid), F32)] + [((block, hid), BF16)] * 3,
        [SMEM, VMEM, VMEM],
        (place, keep, swap(send, "zl", 1)),
    )
    pairs = [swap(p, "zl", 2 * (k + 1)) for k, p in enumerate(pairs)]
    kept, given = call(sum_last, [half] * 2, [VMEM] * 3 + [LATER] * 2, (s0, u, v, *pairs[:2]))
    (grad_weight,) = call(
        functools.partial(sum_scaled, factor=factor),
        [((block, hid), F32)],
        [VMEM] * 4,
        (partial, *pairs),
    )
    given = swap(given, "c", 1)
    (output,) = call(
        interleave,
        [((group // block, 2, block, tokens), BF16)],
        [SMEM, VMEM, VMEM],
        (place, kept.reshape(-1, block, tokens), given.reshape(-1, block, tokens)),
    )
    output = output.reshape(-1, tokens).T
    return (output, grad_pre.T, grad_weight)


def solution(mesh):
    fine = Mesh(np.asarray(mesh.devices).reshape(SIZES), AXES)
    dp, tensor = AXES[:3], AXES[3:]
    mapped = jax.shard_map(
        local,
        mesh=fine,
        in_specs=(P(None, None), P(dp, tensor), P(dp, tensor), P(dp, None)),
        out_specs=(P(dp, tensor), P(dp, tensor), P(dp, tensor)),
        check_vma=False,
    )

    def run(pre_act, weight_out, cotangent):
        block = weight_out.shape[0] // (SIZES[0] * SIZES[1] * SIZES[2])
        k = np.arange(SIZES[1] * block)
        base = (k // block * (2 * block) + k % block).astype(np.int32)[:, None]
        return mapped(jnp.asarray(base), pre_act, weight_out, cotangent)

    return run
```

```python
import functools
import math

import jax
import jax.numpy as jnp
import numpy as np
from jax import lax
from jax.experimental import pallas as pl
from jax.experimental.pallas import tpu as pltpu
from jax.sharding import Mesh, PartitionSpec as P

COEFF = math.sqrt(2.0 / math.pi)
AXES = ("y", "zl", "c", "zh", "x")
SIZES = (4, 8, 2, 4, 4)
F32, BF16 = jnp.float32, jnp.bfloat16
SMEM = pl.BlockSpec(memory_space=pltpu.SMEM)
VMEM = pl.BlockSpec(memory_space=pltpu.VMEM)
LATER = pl.BlockSpec(memory_space=pl.ANY)
HBM = pl.BlockSpec(memory_space=pltpu.HBM)


def gelu_value(values):
    inner = COEFF * (values + 0.044715 * values * values * values)
    return 0.5 * values * (1.0 + jnp.tanh(inner))


def gelu_slope(values):
    tangent = jnp.tanh(COEFF * (values + 0.044715 * values * values * values))
    return 0.5 * (1.0 + tangent) + 0.5 * values * (1.0 - tangent * tangent) * COEFF * (
        1.0 + 3.0 * 0.044715 * values * values
    )


def swap(value, axis, distance):
    size = lax.axis_size(axis)
    return lax.ppermute(value, axis, [(i, i ^ distance) for i in range(size)])


def shift(value, axis, distance):
    size = lax.axis_size(axis)
    return lax.ppermute(value, axis, [(i, (i + distance) % size) for i in range(size)])


def shift_both(value, distance):
    size = lax.axis_size("zh")
    pairs = [
        (core * size + i, core * size + (i + distance * (1 - 2 * core)) % size)
        for core in range(2)
        for i in range(size)
    ]
    return lax.ppermute(value, ("c", "zh"), pairs)


def dot(left, right, over_left, over_right):
    dims = (((over_left,), (over_right,)), ((), ()))
    return lax.dot_general(left, right, dims, preferred_element_type=F32)


def call(body, outs, specs, args, flops=0, scratch=(), out_specs=None, limit=14):
    moved = sum(a.size * a.dtype.itemsize for a in args) + sum(a.size for a in args)
    return pl.pallas_call(
        body,
        out_shape=[s if isinstance(s, pl.MemoryRef) else jax.ShapeDtypeStruct(*s) for s in outs],
        in_specs=specs,
        out_specs=out_specs or [VMEM] * len(outs),
        scratch_shapes=list(scratch),
        compiler_params=pltpu.CompilerParams(vmem_limit_bytes=limit << 20),
        cost_estimate=pl.CostEstimate(flops=flops, bytes_accessed=moved, transcendentals=0),
    )(*args)


def sort_channels(place, base, cot, pre, send, mine, *, block):
    core, stripe = place[0], base.shape[0]
    lanes = lax.broadcasted_iota(jnp.int32, (stripe, 2 * stripe), 1)
    own = jnp.where(lanes == base[...] + core * block, 1.0, 0.0).astype(BF16)
    other = jnp.where(lanes == base[...] + (1 - core) * block, 1.0, 0.0).astype(BF16)
    for index in range(cot.shape[1] // (2 * stripe)):
        part = cot[:, index * 2 * stripe : (index + 1) * 2 * stripe]
        rows = slice(index * stripe, (index + 1) * stripe)
        send[rows, :] = dot(other, part, 1, 1).astype(BF16)
        mine[rows, :] = dot(own, part, 1, 1).astype(BF16)
    send[mine.shape[0] :, :] = pre[...]


def weight_term(place, pre, mine, got, hidden, t0, t1, t2, t3, both, held, sems, *, stripe):
    y, tokens, channels = place[1], pre.shape[1], mine.shape[0]
    copies = [
        pltpu.make_async_copy(mine, both.at[0], sems.at[0]),
        pltpu.make_async_copy(got.at[pl.ds(0, channels)], both.at[1], sems.at[1]),
    ]
    for copy in copies:
        copy.start()
    hidden[:, :tokens] = gelu_value(pre[...].astype(F32)).astype(BF16)
    hidden[:, tokens:] = gelu_value(got[channels:, :].astype(F32)).astype(BF16)
    for index, term in enumerate((t0, t1, t2, t3)):
        rows = pl.ds(pl.multiple_of((y + index) % 4 * stripe, 16), stripe)
        total = dot(mine[rows, :], hidden[:, :tokens], 1, 1)
        total += dot(got[rows, :], hidden[:, tokens:], 1, 1)
        held[index] = total.astype(BF16)
        copies.append(pltpu.make_async_copy(held.at[index], term, sems.at[2 + index]))
        copies[-1].start()
    for copy in copies:
        copy.wait()


def sum_y(p0, p1, p2, p3, after, then, out, held, sem):
    value = p0[...].astype(F32) + p1[...].astype(F32)
    held[...] = (value + (p2[...].astype(F32) + p3[...].astype(F32))).astype(BF16)
    copy = pltpu.make_async_copy(held, out, sem)
    copy.start()
    copy.wait()


def sum_scaled(parts, out, *, factor):
    total = parts[0].astype(F32)
    for index in range(1, parts.shape[0]):
        total += parts[index].astype(F32)
    out[...] = total * factor


def output_terms(place, w0, w1, w2, w3, hidden, out, weight, token, held, sems):
    core, y, zh = place[0], place[1], place[3]
    group = out.shape[2]
    pieces = (w0, w1, w2, w3)
    token[...] = jnp.zeros_like(token)
    copies = [pltpu.make_async_copy(p, weight.at[k], sems.at[k]) for k, p in enumerate(pieces)]
    for copy in copies:
        copy.start()
    for k, piece in enumerate(pieces):
        total = dot(piece[...], hidden[...], 1, 0).astype(BF16)
        target = (y + k - zh + 4) * (1 + 2 * core) % 4
        for x in range(out.shape[0]):
            held[k, x] = total[x * group : (x + 1) * group]
        copies.append(pltpu.make_async_copy(held.at[k], out.at[:, target], sems.at[4 + k]))
        copies[-1].start()
    for copy in copies:
        copy.wait()


def sum_x(parts, after, s0, s1, s2, s3):
    for index, out in enumerate((s0, s1, s2, s3)):
        value = parts[0, index].astype(F32) + parts[1, index].astype(F32)
        value += parts[2, index].astype(F32) + parts[3, index].astype(F32)
        out[...] = value.astype(BF16)


def sum_step(s1, got, t1):
    t1[...] = (s1[...].astype(F32) + got[...].astype(F32)).astype(BF16)


def sum_last(s0, u, v, kept, given):
    half = kept.shape[1]
    total = (s0[...].astype(F32) + (u[...].astype(F32) + v[...].astype(F32))).astype(BF16)
    kept[...] = total[:, :half]
    given[...] = total[:, half:]


def hidden_grad(pre, own, other, out, token):
    token[...] = jnp.zeros_like(token)
    out[...] = ((own[...] + other[...]) * gelu_slope(pre[...].astype(F32))).astype(BF16)


def gate(value, after, out):
    pass


def hold(value, after, place=LATER):
    return pl.pallas_call(
        gate,
        out_shape=pltpu.HBM(value.shape, value.dtype),
        in_specs=[HBM, place],
        out_specs=HBM,
        input_output_aliases={0: 0},
        compiler_params=pltpu.CompilerParams(vmem_limit_bytes=14 << 20),
    )(value, after)


def interleave(place, kept, given, out):
    core = place[0]
    for index in range(kept.shape[0]):
        out[index, core] = kept[index]
        out[index, 1 - core] = given[index]


def hidden_terms(place, weight, both, own, other):
    y, count, stripe = place[1], weight.shape[0], weight.shape[1]
    own[...] = jnp.zeros_like(own)
    other[...] = jnp.zeros_like(other)
    for k in range(count):
        rows = pl.ds(pl.multiple_of((y + k) % count * stripe, 16), stripe)
        own[...] += dot(weight[k], both[0, rows, :], 0, 0)
        other[...] += dot(weight[k], both[1, rows, :], 0, 0)


def local(base, pre_act, weight_out, cotangent):
    n_y, n_zl, n_x = SIZES[0], SIZES[1], SIZES[4]
    tokens, hid = pre_act.shape
    block = weight_out.shape[0]
    stripe = n_zl * block
    group = stripe // n_x
    channels = n_y * stripe
    place = jnp.stack([lax.axis_index(a) for a in ("c", "y", "zl", "zh", "x")]).astype(jnp.int32)
    factor = 1.0 / math.sqrt(tokens * n_y * n_zl * 2)
    work = 2 * tokens * channels * hid * 2
    pre = pre_act.T

    rows = lax.all_to_all(jnp.broadcast_to(weight_out[None], (n_zl, block, hid)), "zl", 0, 0)
    send, mine = call(
        functools.partial(sort_channels, block=block),
        [((channels + hid, tokens), BF16), ((channels, tokens), BF16)],
        [SMEM, VMEM, VMEM, VMEM],
        (place, base, cotangent, pre),
        flops=2 * 4 * tokens * stripe * stripe * 2 * 2,
        limit=56,
    )
    got = swap(send, "c", 1)
    hidden, t0, t1, t2, t3, both = call(
        functools.partial(weight_term, stripe=stripe),
        [((hid, 2 * tokens), BF16)]
        + [pltpu.HBM((stripe, hid), BF16)] * n_y
        + [pltpu.HBM((2, channels, tokens), BF16)],
        [SMEM] + [VMEM] * 3,
        (place, pre, mine, got),
        flops=work,
        scratch=[pltpu.VMEM((n_y, stripe, hid), BF16), pltpu.SemaphoreType.DMA((2 + n_y,))],
        out_specs=[VMEM] + [HBM] * (n_y + 1),
    )

    w0 = rows.reshape(stripe, hid)
    w1, w3, w2 = shift(w0, "y", -1), shift(w0, "y", 1), shift(w0, "y", 2)

    parts, weight, token = call(
        output_terms,
        [pltpu.HBM((n_x, n_y, group, 2 * tokens), BF16), pltpu.HBM((n_y, stripe, hid), BF16), ((8, 128), F32)],
        [SMEM] + [VMEM] * 5,
        (place, w0, w1, w2, w3, hidden),
        flops=work,
        scratch=[pltpu.VMEM((n_y, n_x, group, 2 * tokens), BF16), pltpu.SemaphoreType.DMA((2 * n_y,))],
        out_specs=[HBM, HBM, VMEM],
    )
    t1, t2, t3 = (shift(hold(t, token), "y", k) for k, t in ((1, t1), (2, t2), (3, t3)))
    parts = lax.all_to_all(parts, "x", 0, 0)

    whole, half = ((group, 2 * tokens), BF16), ((group, tokens), BF16)
    terms = [t.reshape(n_zl, block, hid) for t in (t0, t1, t2, t3)]
    own, other = call(
        hidden_terms,
        [((hid, tokens), F32)] * 2,
        [SMEM, VMEM, VMEM],
        (place, weight, both),
        flops=work,
    )
    grad_pre, token = call(
        hidden_grad, [((hid, tokens), BF16), ((8, 128), F32)], [VMEM] * 3, (pre, own, swap(other, "c", 1))
    )
    s0, s1, s2, s3 = call(sum_x, [whole] * 4, [VMEM, LATER], (parts, token))
    got2, v = shift_both(s2, 1), shift_both(s3, -1)
    (t1,) = call(sum_step, [whole], [VMEM] * 2, (s1, got2))
    u = shift_both(t1, 1)
    (term,) = call(
        sum_y,
        [pltpu.HBM((n_zl, block, hid), BF16)],
        [VMEM] * 4 + [LATER] * 2,
        (*terms, t1, v),
        scratch=[pltpu.VMEM((n_zl, block, hid), BF16), pltpu.SemaphoreType.DMA],
        out_specs=[HBM],
    )
    kept, given = call(sum_last, [half] * 2, [VMEM] * 3, (s0, u, v))
    (grad_weight,) = call(
        functools.partial(sum_scaled, factor=factor),
        [((block, hid), F32)],
        [VMEM],
        (lax.all_to_all(hold(term, u), "zl", 0, 0),),
    )
    given = swap(given, "c", 1)
    (output,) = call(
        interleave,
        [((group // block, 2, block, tokens), BF16)],
        [SMEM, VMEM, VMEM],
        (place, kept.reshape(-1, block, tokens), given.reshape(-1, block, tokens)),
    )
    output = output.reshape(-1, tokens).T
    return (output, grad_pre.T, grad_weight)


def solution(mesh):
    fine = Mesh(np.asarray(mesh.devices).reshape(SIZES), AXES)
    dp, tensor = AXES[:3], AXES[3:]
    mapped = jax.shard_map(
        local,
        mesh=fine,
        in_specs=(P(None, None), P(dp, tensor), P(dp, tensor), P(dp, None)),
        out_specs=(P(dp, tensor), P(dp, tensor), P(dp, tensor)),
        check_vma=False,
    )

    def run(pre_act, weight_out, cotangent):
        block = weight_out.shape[0] // (SIZES[0] * SIZES[1] * SIZES[2])
        k = np.arange(SIZES[1] * block)
        base = (k // block * (2 * block) + k % block).astype(np.int32)[:, None]
        return mapped(jnp.asarray(base), pre_act, weight_out, cotangent)

    return run
```

```python
import functools
import math

import jax
import jax.numpy as jnp
import numpy as np
from jax import lax
from jax.experimental import pallas as pl
from jax.experimental.pallas import tpu as pltpu
from jax.sharding import Mesh, PartitionSpec as P

COEFF = math.sqrt(2.0 / math.pi)
AXES = ("y", "zq", "zb", "c", "zh", "x")
SIZES = (4, 4, 2, 2, 4, 4)
F32, BF16 = jnp.float32, jnp.bfloat16
SMEM = pl.BlockSpec(memory_space=pltpu.SMEM)
VMEM = pl.BlockSpec(memory_space=pltpu.VMEM)
LATER = pl.BlockSpec(memory_space=pl.ANY)
HBM = pl.BlockSpec(memory_space=pltpu.HBM)


def gelu_value(values):
    inner = COEFF * (values + 0.044715 * values * values * values)
    return 0.5 * values * (1.0 + jnp.tanh(inner))


def gelu_slope(values):
    tangent = jnp.tanh(COEFF * (values + 0.044715 * values * values * values))
    return 0.5 * (1.0 + tangent) + 0.5 * values * (1.0 - tangent * tangent) * COEFF * (
        1.0 + 3.0 * 0.044715 * values * values
    )


def swap(value, axis, distance):
    size = lax.axis_size(axis)
    return lax.ppermute(value, axis, [(i, i ^ distance) for i in range(size)])


def shift(value, axis, distance):
    size = lax.axis_size(axis)
    return lax.ppermute(value, axis, [(i, (i + distance) % size) for i in range(size)])


def shift_both(value, distance):
    size = lax.axis_size("zh")
    pairs = [
        (core * size + i, core * size + (i + distance * (1 - 2 * core)) % size)
        for core in range(2)
        for i in range(size)
    ]
    return lax.ppermute(value, ("c", "zh"), pairs)


def dot(left, right, over_left, over_right):
    dims = (((over_left,), (over_right,)), ((), ()))
    return lax.dot_general(left, right, dims, preferred_element_type=F32)


def call(body, outs, specs, args, flops=0, scratch=(), out_specs=None, limit=14):
    moved = sum(a.size * a.dtype.itemsize for a in args) + sum(a.size for a in args)
    return pl.pallas_call(
        body,
        out_shape=[s if isinstance(s, pl.MemoryRef) else jax.ShapeDtypeStruct(*s) for s in outs],
        in_specs=specs,
        out_specs=out_specs or [VMEM] * len(outs),
        scratch_shapes=list(scratch),
        compiler_params=pltpu.CompilerParams(vmem_limit_bytes=limit << 20),
        cost_estimate=pl.CostEstimate(flops=flops, bytes_accessed=moved, transcendentals=0),
    )(*args)


def sort_channels(place, base, cot, pre, send, mine, *, block):
    core, stripe = place[0], base.shape[0]
    lanes = lax.broadcasted_iota(jnp.int32, (stripe, 2 * stripe), 1)
    own = jnp.where(lanes == base[...] + core * block, 1.0, 0.0).astype(BF16)
    other = jnp.where(lanes == base[...] + (1 - core) * block, 1.0, 0.0).astype(BF16)
    for index in range(cot.shape[1] // (2 * stripe)):
        part = cot[:, index * 2 * stripe : (index + 1) * 2 * stripe]
        rows = slice(index * stripe, (index + 1) * stripe)
        send[rows, :] = dot(other, part, 1, 1).astype(BF16)
        mine[rows, :] = dot(own, part, 1, 1).astype(BF16)
    send[mine.shape[0] :, :] = pre[...]


def weight_term(place, pre, mine, got, hidden, t0, t1, t2, t3, both, held, sems, *, stripe):
    y, tokens, channels = place[1], pre.shape[1], mine.shape[0]
    copies = [
        pltpu.make_async_copy(mine, both.at[0], sems.at[0]),
        pltpu.make_async_copy(got.at[pl.ds(0, channels)], both.at[1], sems.at[1]),
    ]
    for copy in copies:
        copy.start()
    hidden[:, :tokens] = gelu_value(pre[...].astype(F32)).astype(BF16)
    hidden[:, tokens:] = gelu_value(got[channels:, :].astype(F32)).astype(BF16)
    for index, term in enumerate((t0, t1, t2, t3)):
        rows = pl.ds(pl.multiple_of((y + index) % 4 * stripe, 16), stripe)
        total = dot(mine[rows, :], hidden[:, :tokens], 1, 1)
        total += dot(got[rows, :], hidden[:, tokens:], 1, 1)
        held[index] = total.astype(BF16)
        copies.append(pltpu.make_async_copy(held.at[index], term, sems.at[2 + index]))
        copies[-1].start()
    for copy in copies:
        copy.wait()


def split_y(place, p0, p1, p2, p3, after, then, keep, send):
    bit = place[2]

    def total(index):
        value = p0[index].astype(F32) + p1[index].astype(F32)
        return value + (p2[index].astype(F32) + p3[index].astype(F32))

    for index in range(keep.shape[0]):
        keep[index] = total(2 * index + bit)
        send[index] = total(2 * index + 1 - bit).astype(BF16)


def sum_pair(kept, got, after, out, held, sem):
    held[...] = (kept[...] + got[...].astype(F32)).astype(BF16)
    copy = pltpu.make_async_copy(held, out, sem)
    copy.start()
    copy.wait()


def sum_scaled(parts, out, *, factor):
    total = parts[0].astype(F32)
    for index in range(1, parts.shape[0]):
        total += parts[index].astype(F32)
    out[...] = total * factor


def output_terms(place, w0, w1, w2, w3, hidden, out, weight, token, held, sems):
    core, y, zh = place[0], place[1], place[3]
    group = out.shape[2]
    pieces = (w0, w1, w2, w3)
    token[...] = jnp.zeros_like(token)
    copies = [pltpu.make_async_copy(p, weight.at[k], sems.at[k]) for k, p in enumerate(pieces)]
    for copy in copies:
        copy.start()
    for k, piece in enumerate(pieces):
        total = dot(piece[...], hidden[...], 1, 0).astype(BF16)
        target = (y + k - zh + 4) * (1 + 2 * core) % 4
        for x in range(out.shape[0]):
            held[k, x] = total[x * group : (x + 1) * group]
        copies.append(pltpu.make_async_copy(held.at[k], out.at[:, target], sems.at[4 + k]))
        copies[-1].start()
    for copy in copies:
        copy.wait()


def sum_x(parts, after, s0, s1, s2, s3):
    for index, out in enumerate((s0, s1, s2, s3)):
        value = parts[0, index].astype(F32) + parts[1, index].astype(F32)
        value += parts[2, index].astype(F32) + parts[3, index].astype(F32)
        out[...] = value.astype(BF16)


def sum_step(s1, got, t1):
    t1[...] = (s1[...].astype(F32) + got[...].astype(F32)).astype(BF16)


def sum_last(s0, u, v, kept, given):
    half = kept.shape[1]
    total = (s0[...].astype(F32) + (u[...].astype(F32) + v[...].astype(F32))).astype(BF16)
    kept[...] = total[:, :half]
    given[...] = total[:, half:]


def hidden_grad(pre, own, other, out, token):
    token[...] = jnp.zeros_like(token)
    out[...] = ((own[...] + other[...]) * gelu_slope(pre[...].astype(F32))).astype(BF16)


def gate(value, after, out):
    pass


def hold(value, after, place=LATER):
    return pl.pallas_call(
        gate,
        out_shape=pltpu.HBM(value.shape, value.dtype),
        in_specs=[HBM, place],
        out_specs=HBM,
        input_output_aliases={0: 0},
        compiler_params=pltpu.CompilerParams(vmem_limit_bytes=14 << 20),
    )(value, after)


def interleave(place, kept, given, out):
    core = place[0]
    for index in range(kept.shape[0]):
        out[index, core] = kept[index]
        out[index, 1 - core] = given[index]


def hidden_terms(place, weight, both, own, other):
    y, count, stripe = place[1], weight.shape[0], weight.shape[1]
    own[...] = jnp.zeros_like(own)
    other[...] = jnp.zeros_like(other)
    for k in range(count):
        rows = pl.ds(pl.multiple_of((y + k) % count * stripe, 16), stripe)
        own[...] += dot(weight[k], both[0, rows, :], 0, 0)
        other[...] += dot(weight[k], both[1, rows, :], 0, 0)


def local(base, pre_act, weight_out, cotangent):
    n_y, n_zl, n_x = SIZES[0], SIZES[1] * SIZES[2], SIZES[5]
    tokens, hid = pre_act.shape
    block = weight_out.shape[0]
    stripe = n_zl * block
    group = stripe // n_x
    channels = n_y * stripe
    place = jnp.stack([lax.axis_index(a) for a in ("c", "y", "zb", "zh", "x")]).astype(jnp.int32)
    factor = 1.0 / math.sqrt(tokens * n_y * n_zl * 2)
    work = 2 * tokens * channels * hid * 2
    pre = pre_act.T

    rows = lax.all_to_all(jnp.broadcast_to(weight_out[None], (n_zl, block, hid)), ("zq", "zb"), 0, 0)
    send, mine = call(
        functools.partial(sort_channels, block=block),
        [((channels + hid, tokens), BF16), ((channels, tokens), BF16)],
        [SMEM, VMEM, VMEM, VMEM],
        (place, base, cotangent, pre),
        flops=2 * 4 * tokens * stripe * stripe * 2 * 2,
        limit=56,
    )
    got = swap(send, "c", 1)
    hidden, t0, t1, t2, t3, both = call(
        functools.partial(weight_term, stripe=stripe),
        [((hid, 2 * tokens), BF16)]
        + [pltpu.HBM((stripe, hid), BF16)] * n_y
        + [pltpu.HBM((2, channels, tokens), BF16)],
        [SMEM] + [VMEM] * 3,
        (place, pre, mine, got),
        flops=work,
        scratch=[pltpu.VMEM((n_y, stripe, hid), BF16), pltpu.SemaphoreType.DMA((2 + n_y,))],
        out_specs=[VMEM] + [HBM] * (n_y + 1),
    )

    w0 = rows.reshape(stripe, hid)
    w1, w3, w2 = shift(w0, "y", -1), shift(w0, "y", 1), shift(w0, "y", 2)

    parts, weight, token = call(
        output_terms,
        [pltpu.HBM((n_x, n_y, group, 2 * tokens), BF16), pltpu.HBM((n_y, stripe, hid), BF16), ((8, 128), F32)],
        [SMEM] + [VMEM] * 5,
        (place, w0, w1, w2, w3, hidden),
        flops=work,
        scratch=[pltpu.VMEM((n_y, n_x, group, 2 * tokens), BF16), pltpu.SemaphoreType.DMA((2 * n_y,))],
        out_specs=[HBM, HBM, VMEM],
    )
    t1, t2, t3 = (shift(hold(t, token), "y", k) for k, t in ((1, t1), (2, t2), (3, t3)))
    parts = lax.all_to_all(parts, "x", 0, 0)

    whole, half = ((group, 2 * tokens), BF16), ((group, tokens), BF16)
    terms = [t.reshape(n_zl, block, hid) for t in (t0, t1, t2, t3)]
    own, other = call(
        hidden_terms,
        [((hid, tokens), F32)] * 2,
        [SMEM, VMEM, VMEM],
        (place, weight, both),
        flops=work,
    )
    grad_pre, token = call(
        hidden_grad, [((hid, tokens), BF16), ((8, 128), F32)], [VMEM] * 3, (pre, own, swap(other, "c", 1))
    )
    s0, s1, s2, s3 = call(sum_x, [whole] * 4, [VMEM, LATER], (parts, token))
    got2, v = shift_both(s2, 1), shift_both(s3, -1)
    (t1,) = call(sum_step, [whole], [VMEM] * 2, (s1, got2))
    u = shift_both(t1, 1)
    quarter = SIZES[1]
    keep, send = call(
        split_y,
        [((quarter, block, hid), F32), ((quarter, block, hid), BF16)],
        [SMEM] + [VMEM] * 4 + [LATER] * 2,
        (place, *terms, t1, v),
    )
    (term,) = call(
        sum_pair,
        [pltpu.HBM((quarter, block, hid), BF16)],
        [VMEM] * 2 + [LATER],
        (keep, swap(hold(send, u), "zb", 1), u),
        scratch=[pltpu.VMEM((quarter, block, hid), BF16), pltpu.SemaphoreType.DMA],
        out_specs=[HBM],
    )
    kept, given = call(sum_last, [half] * 2, [VMEM] * 3, (s0, u, v))
    (grad_weight,) = call(
        functools.partial(sum_scaled, factor=factor),
        [((block, hid), F32)],
        [VMEM],
        (lax.all_to_all(term, "zq", 0, 0),),
    )
    given = swap(given, "c", 1)
    (output,) = call(
        interleave,
        [((group // block, 2, block, tokens), BF16)],
        [SMEM, VMEM, VMEM],
        (place, kept.reshape(-1, block, tokens), given.reshape(-1, block, tokens)),
    )
    output = output.reshape(-1, tokens).T
    return (output, grad_pre.T, grad_weight)


def solution(mesh):
    fine = Mesh(np.asarray(mesh.devices).reshape(SIZES), AXES)
    dp, tensor = AXES[:4], AXES[4:]
    mapped = jax.shard_map(
        local,
        mesh=fine,
        in_specs=(P(None, None), P(dp, tensor), P(dp, tensor), P(dp, None)),
        out_specs=(P(dp, tensor), P(dp, tensor), P(dp, tensor)),
        check_vma=False,
    )

    def run(pre_act, weight_out, cotangent):
        block = weight_out.shape[0] // math.prod(SIZES[:4])
        k = np.arange(SIZES[1] * SIZES[2] * block)
        base = (k // block * (2 * block) + k % block).astype(np.int32)[:, None]
        return mapped(jnp.asarray(base), pre_act, weight_out, cotangent)

    return run
```

```python
import functools
import math

import jax
import jax.numpy as jnp
import numpy as np
from jax import lax
from jax.experimental import pallas as pl
from jax.experimental.pallas import tpu as pltpu
from jax.sharding import Mesh, PartitionSpec as P

COEFF = math.sqrt(2.0 / math.pi)
AXES = ("y", "zl", "c", "zh", "x")
SIZES = (4, 8, 2, 4, 4)
F32, BF16 = jnp.float32, jnp.bfloat16
SMEM = pl.BlockSpec(memory_space=pltpu.SMEM)
VMEM = pl.BlockSpec(memory_space=pltpu.VMEM)
LATER = pl.BlockSpec(memory_space=pl.ANY)
HBM = pl.BlockSpec(memory_space=pltpu.HBM)


def gelu_value(values):
    inner = COEFF * (values + 0.044715 * values * values * values)
    return 0.5 * values * (1.0 + jnp.tanh(inner))


def gelu_slope(values):
    tangent = jnp.tanh(COEFF * (values + 0.044715 * values * values * values))
    return 0.5 * (1.0 + tangent) + 0.5 * values * (1.0 - tangent * tangent) * COEFF * (
        1.0 + 3.0 * 0.044715 * values * values
    )


def swap(value, axis, distance):
    size = lax.axis_size(axis)
    return lax.ppermute(value, axis, [(i, i ^ distance) for i in range(size)])


def shift(value, axis, distance):
    size = lax.axis_size(axis)
    return lax.ppermute(value, axis, [(i, (i + distance) % size) for i in range(size)])


def shift_both(value, distance):
    size = lax.axis_size("zh")
    pairs = [
        (core * size + i, core * size + (i + distance * (1 - 2 * core)) % size)
        for core in range(2)
        for i in range(size)
    ]
    return lax.ppermute(value, ("c", "zh"), pairs)


def dot(left, right, over_left, over_right):
    dims = (((over_left,), (over_right,)), ((), ()))
    return lax.dot_general(left, right, dims, preferred_element_type=F32)


def call(body, outs, specs, args, flops=0, scratch=(), out_specs=None, limit=14):
    moved = sum(a.size * a.dtype.itemsize for a in args) + sum(a.size for a in args)
    return pl.pallas_call(
        body,
        out_shape=[s if isinstance(s, pl.MemoryRef) else jax.ShapeDtypeStruct(*s) for s in outs],
        in_specs=specs,
        out_specs=out_specs or [VMEM] * len(outs),
        scratch_shapes=list(scratch),
        compiler_params=pltpu.CompilerParams(vmem_limit_bytes=limit << 20),
        cost_estimate=pl.CostEstimate(flops=flops, bytes_accessed=moved, transcendentals=0),
    )(*args)


def sort_channels(place, base, cot, pre, send, mine, *, block):
    core, stripe = place[0], base.shape[0]
    lanes = lax.broadcasted_iota(jnp.int32, (stripe, 2 * stripe), 1)
    own = jnp.where(lanes == base[...] + core * block, 1.0, 0.0).astype(BF16)
    other = jnp.where(lanes == base[...] + (1 - core) * block, 1.0, 0.0).astype(BF16)
    for index in range(cot.shape[1] // (2 * stripe)):
        part = cot[:, index * 2 * stripe : (index + 1) * 2 * stripe]
        rows = slice(index * stripe, (index + 1) * stripe)
        send[rows, :] = dot(other, part, 1, 1).astype(BF16)
        mine[rows, :] = dot(own, part, 1, 1).astype(BF16)
    send[mine.shape[0] :, :] = pre[...]


def weight_term(place, pre, mine, got, hidden, t0, t1, t2, t3, both, held, sems, *, stripe):
    y, tokens, channels = place[1], pre.shape[1], mine.shape[0]
    copies = [
        pltpu.make_async_copy(mine, both.at[0], sems.at[0]),
        pltpu.make_async_copy(got.at[pl.ds(0, channels)], both.at[1], sems.at[1]),
    ]
    for copy in copies:
        copy.start()
    hidden[:, :tokens] = gelu_value(pre[...].astype(F32)).astype(BF16)
    hidden[:, tokens:] = gelu_value(got[channels:, :].astype(F32)).astype(BF16)
    for index, term in enumerate((t0, t1, t2, t3)):
        rows = pl.ds(pl.multiple_of((y + index) % 4 * stripe, 16), stripe)
        total = dot(mine[rows, :], hidden[:, :tokens], 1, 1)
        total += dot(got[rows, :], hidden[:, tokens:], 1, 1)
        held[index] = total.astype(BF16)
        copies.append(pltpu.make_async_copy(held.at[index], term, sems.at[2 + index]))
        copies[-1].start()
    for copy in copies:
        copy.wait()


def sum_y(p0, p1, p2, p3, after, then, out, held, sem):
    value = p0[...].astype(F32) + p1[...].astype(F32)
    held[...] = (value + (p2[...].astype(F32) + p3[...].astype(F32))).astype(BF16)
    copy = pltpu.make_async_copy(held, out, sem)
    copy.start()
    copy.wait()


def sum_scaled(parts, out, *, factor):
    total = parts[0].astype(F32)
    for index in range(1, parts.shape[0]):
        total += parts[index].astype(F32)
    out[...] = total * factor


def output_terms(place, w0, w1, w2, w3, hidden, out, weight, token, held, sems):
    core, y, zh = place[0], place[1], place[3]
    group = out.shape[2]
    pieces = (w0, w1, w2, w3)
    token[...] = jnp.zeros_like(token)
    copies = [pltpu.make_async_copy(p, weight.at[k], sems.at[k]) for k, p in enumerate(pieces)]
    for copy in copies:
        copy.start()
    for k, piece in enumerate(pieces):
        total = dot(piece[...], hidden[...], 1, 0).astype(BF16)
        target = (y + k - zh + 4) * (1 + 2 * core) % 4
        for x in range(out.shape[0]):
            held[k, x] = total[x * group : (x + 1) * group]
        copies.append(pltpu.make_async_copy(held.at[k], out.at[:, target], sems.at[4 + k]))
        copies[-1].start()
    for copy in copies:
        copy.wait()


def sum_x(parts, after, s0, s1, s2, s3):
    for index, out in enumerate((s0, s1, s2, s3)):
        value = parts[0, index].astype(F32) + parts[1, index].astype(F32)
        value += parts[2, index].astype(F32) + parts[3, index].astype(F32)
        out[...] = value.astype(BF16)


def sum_step(s1, got, t1):
    t1[...] = (s1[...].astype(F32) + got[...].astype(F32)).astype(BF16)


def sum_last(s0, u, v, kept, given):
    half = kept.shape[1]
    total = (s0[...].astype(F32) + (u[...].astype(F32) + v[...].astype(F32))).astype(BF16)
    kept[...] = total[:, :half]
    given[...] = total[:, half:]


def hidden_grad(pre, own, other, out, token):
    token[...] = jnp.zeros_like(token)
    out[...] = ((own[...] + other[...]) * gelu_slope(pre[...].astype(F32))).astype(BF16)


def gate(value, after, out):
    pass


def hold(value, after, place=LATER):
    return pl.pallas_call(
        gate,
        out_shape=pltpu.HBM(value.shape, value.dtype),
        in_specs=[HBM, place],
        out_specs=HBM,
        input_output_aliases={0: 0},
        compiler_params=pltpu.CompilerParams(vmem_limit_bytes=14 << 20),
    )(value, after)


def interleave(place, kept, given, out):
    core = place[0]
    for index in range(kept.shape[0]):
        out[index, core] = kept[index]
        out[index, 1 - core] = given[index]


def hidden_terms(place, weight, both, own, other):
    y, count, stripe = place[1], weight.shape[0], weight.shape[1]
    own[...] = jnp.zeros_like(own)
    other[...] = jnp.zeros_like(other)
    for k in range(count):
        rows = pl.ds(pl.multiple_of((y + k) % count * stripe, 16), stripe)
        own[...] += dot(weight[k], both[0, rows, :], 0, 0)
        other[...] += dot(weight[k], both[1, rows, :], 0, 0)


def local(base, pre_act, weight_out, cotangent):
    n_y, n_zl, n_x = SIZES[0], SIZES[1], SIZES[4]
    tokens, hid = pre_act.shape
    block = weight_out.shape[0]
    stripe = n_zl * block
    group = stripe // n_x
    channels = n_y * stripe
    place = jnp.stack([lax.axis_index(a) for a in ("c", "y", "zl", "zh", "x")]).astype(jnp.int32)
    factor = 1.0 / math.sqrt(tokens * n_y * n_zl * 2)
    work = 2 * tokens * channels * hid * 2
    pre = pre_act.T

    rows = lax.all_to_all(jnp.broadcast_to(weight_out[None], (n_zl, block, hid)), "zl", 0, 0)
    send, mine = call(
        functools.partial(sort_channels, block=block),
        [((channels + hid, tokens), BF16), ((channels, tokens), BF16)],
        [SMEM, VMEM, VMEM, VMEM],
        (place, base, cotangent, pre),
        flops=2 * 4 * tokens * stripe * stripe * 2 * 2,
        limit=56,
    )
    got = swap(send, "c", 1)
    hidden, t0, t1, t2, t3, both = call(
        functools.partial(weight_term, stripe=stripe),
        [((hid, 2 * tokens), BF16)]
        + [pltpu.HBM((stripe, hid), BF16)] * n_y
        + [pltpu.HBM((2, channels, tokens), BF16)],
        [SMEM] + [VMEM] * 3,
        (place, pre, mine, got),
        flops=work,
        scratch=[pltpu.VMEM((n_y, stripe, hid), BF16), pltpu.SemaphoreType.DMA((2 + n_y,))],
        out_specs=[VMEM] + [HBM] * (n_y + 1),
    )

    w0 = rows.reshape(stripe, hid)
    w1, w3, w2 = shift(w0, "y", -1), shift(w0, "y", 1), shift(w0, "y", 2)

    parts, weight, token = call(
        output_terms,
        [pltpu.HBM((n_x, n_y, group, 2 * tokens), BF16), pltpu.HBM((n_y, stripe, hid), BF16), ((8, 128), F32)],
        [SMEM] + [VMEM] * 5,
        (place, w0, w1, w2, w3, hidden),
        flops=work,
        scratch=[pltpu.VMEM((n_y, n_x, group, 2 * tokens), BF16), pltpu.SemaphoreType.DMA((2 * n_y,))],
        out_specs=[HBM, HBM, VMEM],
    )
    t1, t2, t3 = (shift(hold(t, token), "y", k) for k, t in ((1, t1), (2, t2), (3, t3)))
    parts = lax.all_to_all(parts, "x", 0, 0)

    whole, half = ((group, 2 * tokens), BF16), ((group, tokens), BF16)
    terms = [t.reshape(n_zl, block, hid) for t in (t0, t1, t2, t3)]
    own, other = call(
        hidden_terms,
        [((hid, tokens), F32)] * 2,
        [SMEM, VMEM, VMEM],
        (place, weight, both),
        flops=work,
        limit=56,
    )
    grad_pre, token = call(
        hidden_grad, [((hid, tokens), BF16), ((8, 128), F32)], [VMEM] * 3, (pre, own, swap(other, "c", 1))
    )
    s0, s1, s2, s3 = call(sum_x, [whole] * 4, [VMEM, LATER], (parts, token))
    got2, v = shift_both(s2, 1), shift_both(s3, -1)
    (t1,) = call(sum_step, [whole], [VMEM] * 2, (s1, got2))
    u = shift_both(t1, 1)
    (term,) = call(
        sum_y,
        [pltpu.HBM((n_zl, block, hid), BF16)],
        [VMEM] * 4 + [LATER] * 2,
        (*terms, t1, v),
        scratch=[pltpu.VMEM((n_zl, block, hid), BF16), pltpu.SemaphoreType.DMA],
        out_specs=[HBM],
    )
    kept, given = call(sum_last, [half] * 2, [VMEM] * 3, (s0, u, v))
    (grad_weight,) = call(
        functools.partial(sum_scaled, factor=factor),
        [((block, hid), F32)],
        [VMEM],
        (lax.all_to_all(hold(term, u), "zl", 0, 0),),
    )
    given = swap(given, "c", 1)
    (output,) = call(
        interleave,
        [((group // block, 2, block, tokens), BF16)],
        [SMEM, VMEM, VMEM],
        (place, kept.reshape(-1, block, tokens), given.reshape(-1, block, tokens)),
    )
    output = output.reshape(-1, tokens).T
    return (output, grad_pre.T, grad_weight)


def solution(mesh):
    fine = Mesh(np.asarray(mesh.devices).reshape(SIZES), AXES)
    dp, tensor = AXES[:3], AXES[3:]
    mapped = jax.shard_map(
        local,
        mesh=fine,
        in_specs=(P(None, None), P(dp, tensor), P(dp, tensor), P(dp, None)),
        out_specs=(P(dp, tensor), P(dp, tensor), P(dp, tensor)),
        check_vma=False,
    )

    def run(pre_act, weight_out, cotangent):
        block = weight_out.shape[0] // (SIZES[0] * SIZES[1] * SIZES[2])
        k = np.arange(SIZES[1] * block)
        base = (k // block * (2 * block) + k % block).astype(np.int32)[:, None]
        return mapped(jnp.asarray(base), pre_act, weight_out, cotangent)

    return run
```
